256 devices in a mesh: wide: 32 (over y, x, core), narrow: 8 (over z).
Axes of the slice: x: 4, y: 4, z: 8, core: 2. Of those that a mesh axis runs over, the one named last changes fastest.
Arguments:
- resid: float32 [4, 2359296], P(None, ('wide', 'narrow')), may hold values from -6 to 6
- mult: int32 [2359296], P(('wide', 'narrow')), may hold values from 1 to 8
- dirichlet_inv: bfloat16 [6144, 384, 384], P(('wide', 'narrow')), may hold values from -0.3125 to 0.3125
- fine_basis: bfloat16 [2359296, 128], P(('wide', 'narrow')), may hold values from -0.1875 to 0.1875
- fine_index: int32 [256, 128], P(('wide', 'narrow')), may hold values from -1 to 511, as said below
- level2_inv: bfloat16 [16384, 512], P('wide'), may hold values from -0.25 to 0.25
- level2_basis: bfloat16 [16384, 128], P('wide'), may hold values from -0.375 to 0.375
- coarse_index: int32 [32, 128], P('wide'), may hold values from 0 to 2047, as said below
- coarse_inv: bfloat16 [2048, 2048], P('wide'), may hold values from -0.25 to 0.25
Outputs:
- correction: float32 [4, 2359296], P(None, ('wide', 'narrow'))
The draws below stay inside these ranges and needn't reach their ends.
Inputs may be any that keep to these rules, and one draw needn't show every extreme that they name: `fine_index`: row s lists the level-2 positions of fine subdomain s's primal unknowns: at least 64 valid entries from the start, then -1 as padding; entries may repeat. `coarse_index`: entries may repeat within a row.
All inputs are finite; a program needn't handle non-finite values.
Results may differ from the reference program's by a relative error of at most 0.02.
Values may be sent and summed in bfloat16 or wider, within the bound.
No kernel may reach another device: no remote copies, remote signals or barrier semaphores. Data moves between devices by JAX's collectives and lax.ppermute only.
A program may use at most 64 MiB of HBM per device.

```python
import jax
import jax.numpy as jnp
from jax import lax

LOADS = 4
BS = 384
NBLK = 24
NP = 128
NP2 = 512
NC2 = 128
NF = 1152
ND = 9216
NC3 = 2048
FINE = 256
L2 = 32
N_NARROW = 8


def draw_fine_index(key, part):
    key = jax.random.fold_in(key, 11)
    key_values, key_lengths = jax.random.split(key)
    values = jax.random.randint(key_values, (FINE, NP), 0, NP2)
    lengths = jax.random.randint(key_lengths, (FINE, 1), NP // 2, NP + 1)
    lengths = lengths.at[0, 0].set(NP).at[1, 0].set(NP // 2)
    values = values.at[0, 0].set(NP2 - 1)
    position = jnp.arange(NP)[None, :]
    return jnp.where(position < lengths, values, -1).astype(jnp.int32)


def draw_coarse_index(key, part):
    key = jax.random.fold_in(key, 23)
    values = jax.random.randint(key, (L2, NC2), 0, NC3)
    values = values.at[0, 0].set(NC3 - 1).at[0, 1].set(0)
    return values.astype(jnp.int32)


def with_ends(entries, key, smallest, largest):
    extent = entries.shape
    index_at = [jax.random.randint(jax.random.fold_in(key, axis), (), 0, extent[axis]) for axis in range(len(extent))]
    entries = entries.at[tuple(index_at)].set(smallest)
    longest = extent.index(max(extent))
    index_at[longest] = (index_at[longest] + 1) % extent[longest]
    return entries.at[tuple(index_at)].set(largest)


def steps_of(stream_key, dims, cuts, least, top_value):
    level, own = 1.0, jax.random.fold_in(stream_key, 6)
    for axis_at, parts in cuts:
        heights = jnp.exp(jax.random.uniform(jax.random.fold_in(own, axis_at), (parts,), jnp.float32, least / len(cuts), top_value / len(cuts)))
        level = level * jnp.repeat(heights, dims[axis_at] // parts).reshape([-1 if axis == axis_at else 1 for axis in range(len(dims))])
    return level


def scatter_about(own_key, dims, spread, limit, shards=(), held_as=jnp.bfloat16):
    drawn = spread * jax.random.normal(own_key, dims, jnp.float32)
    if shards:
        drawn = drawn * steps_of(own_key, dims, shards, -0.22, 0.18)
    return jnp.clip(drawn, -limit, limit).astype(held_as)


def setup_inputs(seed: int = 0) -> dict:
    key_list = jax.random.split(jax.random.key(seed), 10)
    return {
        "resid": scatter_about(key_list[0], (LOADS, FINE * ND), 1.0, 6.0, ((1, 256),), jnp.float32),
        "mult": with_ends(jax.random.randint(key_list[1], (FINE * ND,), 1, 9), jax.random.fold_in(key_list[1], 1), 1, 8).astype(jnp.int32),
        "dirichlet_inv": scatter_about(key_list[2], (FINE * NBLK, BS, BS), BS ** -0.5, 0.3125, ((0, 256),)),
        "fine_basis": scatter_about(key_list[3], (FINE * ND, NP), (8 * NP) ** -0.5, 0.1875, ((0, 256),)),
        "fine_index": draw_fine_index(jax.random.fold_in(key_list[9], 71), 0),
        "level2_inv": scatter_about(key_list[5], (L2 * NP2, NP2), NP2 ** -0.5, 0.25, ((0, 32),)),
        "level2_basis": scatter_about(key_list[6], (L2 * NP2, NC2), (2 * NC2) ** -0.5, 0.375, ((0, 32),)),
        "coarse_index": draw_coarse_index(jax.random.fold_in(key_list[9], 71), 0),
        "coarse_inv": scatter_about(key_list[8], (NC3, NC3), (NC3 // 4) ** -0.5, 0.25, ((0, 32),)),
    }


def reference(resid, mult, dirichlet_inv, fine_basis, fine_index, level2_inv, level2_basis, coarse_index, coarse_inv):
    highest = lax.Precision.HIGHEST
    res_sub = resid.reshape(LOADS, FINE, ND).transpose(1, 0, 2)
    mul_sub = mult.reshape(FINE, ND).astype(jnp.float32)
    inv_sub = dirichlet_inv.reshape(FINE, NBLK, BS, BS)
    basis_sub = fine_basis.reshape(FINE, ND, NP)

    def descend(item):
        values, weights, blocks, basis = item
        weighted = (values / weights[None, :]).astype(jnp.bfloat16)
        interior = jnp.einsum("bij,kbj->kbi", blocks.astype(jnp.float32), weighted.reshape(LOADS, NBLK, BS).astype(jnp.float32), precision=highest).reshape(LOADS, ND)
        primal = jnp.dot(weighted, basis, preferred_element_type=jnp.float32)
        return interior, primal

    interior, fine_primal = lax.map(descend, (res_sub, mul_sub, inv_sub, basis_sub))
    select = (fine_index[:, :, None] == jnp.arange(NP2, dtype=jnp.int32)[None, None, :]).astype(jnp.float32)
    contrib = jnp.einsum("skp,spm->skm", fine_primal, select, precision=highest)
    level2_resid = contrib.reshape(L2, N_NARROW, LOADS, NP2).sum(axis=1)
    level2_low = level2_resid.astype(jnp.bfloat16).astype(jnp.float32)
    inv_two = level2_inv.reshape(L2, NP2, NP2).astype(jnp.float32)
    basis_two = level2_basis.reshape(L2, NP2, NC2).astype(jnp.float32)
    level2_local = jnp.einsum("gkj,gij->gki", level2_low, inv_two, precision=highest)
    level2_primal = jnp.einsum("gkm,gmc->gkc", level2_low, basis_two, precision=highest)
    pick_two = (coarse_index[:, :, None] == jnp.arange(NC3, dtype=jnp.int32)[None, None, :]).astype(jnp.float32)
    coarse_resid = jnp.einsum("gkc,gct->kt", level2_primal, pick_two, precision=highest)
    coarse_low = coarse_resid.astype(jnp.bfloat16)
    coarse_corr = jnp.dot(coarse_low, coarse_inv.T, preferred_element_type=jnp.float32).astype(jnp.bfloat16)
    picked = jnp.einsum("kt,gct->gkc", coarse_corr.astype(jnp.float32), pick_two, precision=highest)
    level2_corr = (level2_local + jnp.einsum("gkc,gmc->gkm", picked, basis_two, precision=highest)).astype(jnp.bfloat16)
    group_corr = jnp.repeat(level2_corr.astype(jnp.float32), N_NARROW, axis=0)
    gathered = jnp.einsum("skm,spm->skp", group_corr, select, precision=highest).astype(jnp.bfloat16)

    def ascend(item):
        inner, picks, basis, weights = item
        fine_corr = inner + jnp.dot(picks, basis.T, preferred_element_type=jnp.float32)
        return fine_corr / weights[None, :]

    scaled = lax.map(ascend, (interior, gathered, basis_sub, mul_sub))
    zeros_front = jnp.zeros((N_NARROW, LOADS, NF), jnp.float32)
    lower = jnp.concatenate([zeros_front, scaled[:-N_NARROW, :, ND - NF:]], axis=0)
    upper = jnp.concatenate([scaled[N_NARROW:, :, :NF], zeros_front], axis=0)
    result = scaled.at[:, :, :NF].add(lower).at[:, :, ND - NF:].add(upper)
    return result.transpose(1, 0, 2).reshape(LOADS, FINE * ND)
```

```python
import jax
import jax.numpy as jnp
from jax import lax
from jax.sharding import PartitionSpec as P

NF = 1152


def spread(chunk, axis):
    count = lax.axis_size(axis)
    return lax.all_to_all(jnp.broadcast_to(chunk[None], (count,) + chunk.shape), axis, 0, 0)


def per_device(
    resid,
    mult,
    dirichlet_inv,
    fine_basis,
    fine_index,
    level2_inv,
    level2_basis,
    coarse_index,
    coarse_inv,
):
    f32, bf16 = jnp.float32, jnp.bfloat16
    highest = lax.Precision.HIGHEST
    loads, width = resid.shape
    blocks, block_size = dirichlet_inv.shape[0], dirichlet_inv.shape[1]
    level_width = level2_inv.shape[1]
    coarse_width = coarse_inv.shape[1]
    rows = coarse_inv.shape[0]
    count = lax.axis_size("wide")

    inverse = (1.0 / mult.astype(f32))[None, :]
    weighted = (resid * inverse).astype(bf16)
    fine_primal = jnp.dot(weighted, fine_basis, preferred_element_type=f32)
    select = fine_index.reshape(-1, 1) == jnp.arange(level_width, dtype=jnp.int32)[None, :]
    contrib = jnp.dot(fine_primal, select.astype(f32), precision=highest)

    level2_low = jnp.sum(spread(contrib, "narrow"), axis=0).astype(bf16)
    interior = jnp.einsum(
        "bij,kbj->kbi",
        dirichlet_inv,
        weighted.reshape(loads, blocks, block_size),
        preferred_element_type=f32,
    ).reshape(loads, width)
    level2_local = jnp.einsum("kj,ij->ki", level2_low, level2_inv, preferred_element_type=f32)
    level2_primal = jnp.dot(level2_low, level2_basis, preferred_element_type=f32)

    own_high = coarse_index // 128
    own_low = coarse_index % 128
    packet = jnp.concatenate(
        [level2_primal.astype(bf16), own_high.astype(bf16), own_low.astype(bf16), jnp.zeros((2, 128), bf16)], axis=0
    )
    packets = spread(packet, "wide")
    high = packets[:, loads : loads + 1, :]
    low = packets[:, loads + 1, :].reshape(1, -1)
    tall = jnp.concatenate(
        [jnp.where(high == jnp.asarray(h, bf16), packets[:, :loads], jnp.zeros((), bf16)) for h in range(coarse_width // 128)],
        axis=1,
    )
    tall = jnp.swapaxes(tall, 0, 1).reshape(-1, count * 128)
    one_hot = (low == jnp.arange(128, dtype=bf16)[:, None]).astype(bf16)
    coarse_resid = lax.dot_general(tall, one_hot, (((1,), (1,)), ((), ())), preferred_element_type=f32)
    coarse_low = jnp.swapaxes(coarse_resid.reshape(-1, loads, 128), 0, 1).reshape(loads, coarse_width).astype(bf16)
    own_rows = jnp.einsum("kj,ij->ki", coarse_low, coarse_inv, preferred_element_type=f32).astype(bf16)

    corr = spread(own_rows, "wide")
    pick_low = (coarse_index % rows == jnp.arange(rows, dtype=jnp.int32)[:, None]).astype(bf16)
    picks = jnp.dot(corr.reshape(count * loads, rows), pick_low, preferred_element_type=f32)
    mask = (coarse_index // rows)[None] == jnp.arange(count, dtype=jnp.int32)[:, None, None]
    picked = jnp.sum(jnp.where(mask, picks.reshape(count, loads, 128), 0.0), axis=0).astype(bf16)
    level2_corr = (
        level2_local + jnp.einsum("kc,mc->km", picked, level2_basis, preferred_element_type=f32)
    ).astype(bf16)
    gathered = jnp.einsum(
        "km,pm->kp", level2_corr, select.astype(bf16), preferred_element_type=f32
    ).astype(bf16)
    scaled = (
        interior + jnp.einsum("kp,dp->kd", gathered, fine_basis, preferred_element_type=f32)
    ) * inverse

    head = scaled[:, :NF].astype(bf16)
    tail = scaled[:, width - NF :].astype(bf16)
    even = lax.axis_index("wide") % 2 == 0
    near = [(i, i ^ 1) for i in range(count)]
    far = [(i, ((i + 1) ^ 1) - 1) for i in range(1, count - 1)]
    from_near = lax.ppermute(jnp.where(even, tail, head), "wide", near)
    from_far = lax.ppermute(jnp.where(even, head, tail), "wide", far)
    to_head = jnp.where(even, from_far, from_near).astype(f32)
    to_tail = jnp.where(even, from_near, from_far).astype(f32)
    return jnp.concatenate(
        [scaled[:, :NF] + to_head, scaled[:, NF : width - NF], scaled[:, width - NF :] + to_tail], axis=1
    )


def solution(mesh):
    placed = (
        P(None, ("wide", "narrow")),
        P(("wide", "narrow")),
        P(("wide", "narrow"), None, None),
        P(("wide", "narrow"), None),
        P(("wide", "narrow"), None),
        P("wide", None),
        P("wide", None),
        P("wide", None),
        P("wide", None),
    )
    return jax.shard_map(
        per_device,
        mesh=mesh,
        in_specs=placed,
        out_specs=P(None, ("wide", "narrow")),
        check_vma=False,
    )
```

```python
import functools

import jax
import jax.numpy as jnp
from jax import lax
from jax.experimental import pallas as pl
from jax.experimental.pallas import tpu as pltpu
from jax.sharding import PartitionSpec as P

NF = 1152
LANES = 128
F32 = jnp.float32
BF16 = jnp.bfloat16
LIMIT = 16 * 1024 * 1024
NN = (((1,), (0,)), ((), ()))
NT = (((1,), (1,)), ((), ()))
VMEM = pl.BlockSpec(memory_space=pltpu.VMEM)


def mm(a, b, dims=NN):
    return lax.dot_general(a, b, dims, preferred_element_type=F32)


def split_mm(a, b, dims=NN):
    high = a.astype(BF16)
    rest = a - high.astype(F32)
    mid = rest.astype(BF16)
    low = (rest - mid.astype(F32)).astype(BF16)
    return mm(high, b, dims) + (mm(mid, b, dims) + mm(low, b, dims))


def selector(index_row, width):
    column = jnp.transpose(jnp.broadcast_to(index_row.astype(F32), (LANES, LANES)))
    lane = lax.broadcasted_iota(jnp.int32, (LANES, LANES), 1).astype(F32)
    return jnp.concatenate(
        [jnp.where(column == lane + float(q * LANES), 1.0, 0.0) for q in range(width // LANES)], axis=1
    ).astype(BF16)


def sides(width):
    me = lax.axis_index("wide")
    odd = lax.rem(me, 2)
    last = width - NF
    near = me + 1 - 2 * odd
    far = jnp.clip(me - 1 + 2 * odd, 0, lax.axis_size("wide") - 1)
    return (pl.multiple_of(last * (1 - odd), LANES), near), (pl.multiple_of(last * odd, LANES), far)


def copies_of(pairs, sems):
    copies = [pltpu.make_async_copy(source, target, sems.at[at]) for at, (source, target) in enumerate(pairs)]
    for copy in copies:
        copy.start()
    return copies


def head_kernel(
    resid_hbm,
    mult_hbm,
    basis_hbm,
    index_hbm,
    basis_ref,
    weighted_ref,
    weight_ref,
    inverse_ref,
    send_ref,
    resid_ref,
    mult_ref,
    index_ref,
    sems,
):
    width = resid_ref.shape[1]
    level_width = 4 * LANES
    parts = sems.shape[0] - 3
    step = width // parts
    cuts = [slice(part * step, (part + 1) * step) for part in range(parts)]
    copies = copies_of(
        [(mult_hbm, mult_ref), (resid_hbm, resid_ref), (index_hbm, index_ref)]
        + [(basis_hbm.at[cut], basis_ref.at[cut]) for cut in cuts],
        sems,
    )
    copies[0].wait()
    weight = mult_ref[...].astype(F32)
    weight_ref[...] = weight
    inverse = 1.0 / weight
    inverse_ref[...] = inverse
    copies[1].wait()
    weighted = (resid_ref[...] * inverse).astype(BF16)
    weighted_ref[...] = weighted
    copies[2].wait()
    select = selector(index_ref[...], level_width)
    total = jnp.zeros((resid_ref.shape[0], LANES), F32)
    for part, cut in enumerate(cuts):
        copies[3 + part].wait()
        total += mm(weighted[:, cut], basis_ref[cut, :])
    contrib = split_mm(total, select)
    chunk = jnp.concatenate(
        [contrib[:, q * LANES : (q + 1) * LANES] for q in range(level_width // LANES)], axis=0
    ).astype(BF16)
    for other in range(send_ref.shape[0]):
        send_ref[other] = chunk


def interior_kernel(weighted_ref, blocks_hbm, interior_ref, blocks_ref, sems, *, depth):
    count, size = blocks_ref.shape[0], blocks_ref.shape[1]

    def copy(b):
        return pltpu.make_async_copy(blocks_hbm.at[b], blocks_ref.at[b], sems.at[b])

    for b in range(depth):
        copy(b).start()
    for b in range(count):
        copy(b).wait()
        if b + depth < count:
            copy(b + depth).start()
        cut = slice(b * size, (b + 1) * size)
        interior_ref[:, cut] = mm(weighted_ref[:, cut], blocks_ref[b], NT)


def level2_kernel(
    parts_ref,
    inverse_ref,
    level2_basis_ref,
    index_ref,
    coarse_index_ref,
    interior_ref,
    weight_ref,
    basis_ref,
    local_ref,
    send_ref,
    picked_ref,
    near_ref,
    far_ref,
    packet,
    stage,
):
    loads, width = interior_ref.shape
    total = jnp.sum(parts_ref[...].astype(F32), axis=0)
    low = jnp.concatenate([total[q * loads : (q + 1) * loads] for q in range(total.shape[0] // loads)], axis=1).astype(BF16)
    local = mm(low, inverse_ref[...], NT)
    select = selector(index_ref[...], level2_basis_ref.shape[0])
    chosen = mm(select, level2_basis_ref[...]).astype(BF16)
    picked_ref[...] = chosen
    local_picked = split_mm(local, select, NT)
    coarse = coarse_index_ref[...]
    packet[...] = jnp.zeros_like(packet)
    packet[:loads, :] = mm(low, level2_basis_ref[...])
    packet[loads : 2 * loads, :] = local_picked
    packet[8:9, :] = (coarse // LANES).astype(F32)
    packet[9:10, :] = (coarse % LANES).astype(F32)
    local_ref[...] = packet[...]
    chunk = packet[...].astype(BF16)
    for other in range(send_ref.shape[0]):
        send_ref[other] = chunk

    pieces = NF // LANES
    for out_ref, (start, _) in zip((near_ref, far_ref), sides(width)):
        out_ref[:NF, :] = basis_ref[pl.ds(start, NF), :]
        out_ref[NF : NF + LANES, :] = chosen
        stage[loads * pieces :, :] = jnp.zeros((stage.shape[0] - loads * pieces, LANES), F32)
        for q in range(pieces):
            lanes = pl.ds(pl.multiple_of(start + q * LANES, LANES), LANES)
            stage[q * loads : (q + 1) * loads, :] = interior_ref[:, lanes]
            stage[loads * pieces + q : loads * pieces + q + 1, :] = weight_ref[:, lanes]
        out_ref[NF + LANES :, :] = stage[...].astype(BF16)


def coarse_kernel(packets_ref, inverse_ref, coarse_index_ref, send_ref, hot_ref, owner_ref, *, width):
    groups = packets_ref.shape[0]
    half = inverse_ref.shape[0]
    highs = inverse_ref.shape[1] // LANES
    row = lax.broadcasted_iota(jnp.int32, (LANES, LANES), 0).astype(F32)
    tall, hot = [], []
    for g in range(groups):
        packet = packets_ref[g].astype(F32)
        values = packet[:8]
        high = jnp.broadcast_to(packet[8:9], (8, LANES))
        tall.append(jnp.concatenate([jnp.where(high == float(h), values, 0.0) for h in range(highs)], axis=0).astype(BF16))
        hot.append(jnp.where(row == jnp.broadcast_to(packet[9:10], (LANES, LANES)), 1.0, 0.0).astype(BF16))
    total = mm(jnp.concatenate(tall, axis=1), jnp.concatenate(hot, axis=1), NT)
    coarse_low = jnp.concatenate([total[8 * h : 8 * h + 8] for h in range(highs)], axis=1).astype(BF16)
    own = mm(coarse_low, inverse_ref[...], NT)
    own = jnp.concatenate([own, jnp.zeros((8, LANES - half), F32)], axis=1)
    chunk = jnp.concatenate([own, jnp.zeros((8, LANES), F32)], axis=0).astype(BF16)
    for other in range(groups):
        send_ref[other] = chunk

    packets = [packets_ref[group].astype(F32) for _, group in sides(width)]
    places = [coarse_index_ref[...].astype(F32)] + [p[8:9] * float(LANES) + p[9:10] for p in packets]
    place = jnp.concatenate(places, axis=1).astype(jnp.int32)
    shape = (LANES, place.shape[1])
    lane = lax.broadcasted_iota(jnp.int32, shape, 0)
    hot_ref[...] = jnp.where(lane == jnp.broadcast_to(place % half, shape), 1.0, 0.0).astype(BF16)
    owner_ref[...] = jnp.broadcast_to(place // half, owner_ref.shape)


def tail_kernel(
    corr_ref,
    packets_ref,
    hot_ref,
    owner_ref,
    local_ref,
    picked_ref,
    near_ref,
    far_ref,
    interior_ref,
    inverse_ref,
    basis_ref,
    out_hbm,
    out_ref,
    sems,
):
    loads, width = interior_ref.shape
    groups = corr_ref.shape[0]
    table = jnp.concatenate([corr_ref[g].astype(F32)[:8] for g in range(groups)], axis=0).astype(BF16)
    picks = mm(table, hot_ref[...])
    owner = owner_ref[...]
    picked = jnp.zeros(owner.shape, F32)
    for g in range(groups):
        picked += jnp.where(owner == g, picks[8 * g : 8 * g + 8], 0.0)
    picked = picked.astype(BF16)
    gathered = (local_ref[4:8, :] + mm(picked[:, :LANES], picked_ref[...], NT)[:loads]).astype(BF16)

    def piece(cut):
        out_ref[:, cut] = (interior_ref[:, cut] + mm(gathered, basis_ref[cut, :], NT)) * inverse_ref[:, cut]

    def send(cut, at):
        copy = pltpu.make_async_copy(out_ref.at[:, cut], out_hbm.at[:, cut], sems.at[at])
        copy.start()
        return copy

    copies = []
    middle = width - 2 * NF
    step = middle // 2
    for at in range(2):
        cut = slice(NF + at * step, NF + (at + 1) * step)
        piece(cut)
        copies.append(send(cut, at))
    ends = [slice(0, NF), slice(width - NF, width)]
    for cut in ends:
        piece(cut)
    pieces = NF // LANES
    for side, (face_ref, (start, group)) in enumerate(zip((near_ref, far_ref), sides(width))):
        lanes = slice((side + 1) * LANES, (side + 2) * LANES)
        packet = packets_ref[group].astype(F32)
        theirs = (packet[4:8] + mm(picked[:, lanes], face_ref[NF : NF + LANES, :], NT)[:loads]).astype(BF16)
        shift = mm(theirs, face_ref[:NF, :], NT)
        rest = face_ref[NF + LANES :, :].astype(F32)
        weight = rest[loads * pieces : loads * pieces + pieces]
        scale = jnp.where(weight > 0.0, 1.0 / jnp.maximum(weight, 1.0), 0.0)
        for q in range(pieces):
            face = (rest[q * loads : (q + 1) * loads] + shift[:, q * LANES : (q + 1) * LANES]) * scale[q : q + 1]
            at = pl.ds(pl.multiple_of(start + q * LANES, LANES), LANES)
            out_ref[:, at] = out_ref[:, at] + face
    for at, cut in enumerate(ends):
        copies.append(send(cut, 2 + at))
    for copy in copies:
        copy.wait()


def params(limit=LIMIT):
    return pltpu.CompilerParams(vmem_limit_bytes=limit)


def per_device(
    resid,
    mult,
    dirichlet_inv,
    fine_basis,
    fine_index,
    level2_inv,
    level2_basis,
    coarse_index,
    coarse_inv,
):
    loads, width = resid.shape
    blocks, size = dirichlet_inv.shape[0], dirichlet_inv.shape[1]
    wide, narrow = lax.axis_size("wide"), lax.axis_size("narrow")
    mult = mult.reshape(1, width)
    rest_rows = 48

    pieces = 4
    hbm = pl.BlockSpec(memory_space=pltpu.HBM)

    def pinned(*arrays):
        return [pltpu.with_memory_space_constraint(array, pltpu.HBM) for array in arrays]

    basis, weighted, weight, inverse, send = pl.pallas_call(
        head_kernel,
        out_shape=(
            jax.ShapeDtypeStruct(fine_basis.shape, BF16),
            jax.ShapeDtypeStruct((loads, width), BF16),
            jax.ShapeDtypeStruct((1, width), F32),
            jax.ShapeDtypeStruct((1, width), F32),
            jax.ShapeDtypeStruct((narrow, 16, LANES), BF16),
        ),
        in_specs=[hbm] * 4,
        out_specs=(VMEM,) * 5,
        scratch_shapes=[
            pltpu.VMEM(resid.shape, F32),
            pltpu.VMEM(mult.shape, jnp.int32),
            pltpu.VMEM(fine_index.shape, jnp.int32),
            pltpu.SemaphoreType.DMA((3 + pieces,)),
        ],
        compiler_params=params(),
        name="head",
    )(*pinned(resid, mult, fine_basis, fine_index))
    parts = lax.all_to_all(send, "narrow", 0, 0)
    interior = pl.pallas_call(
        functools.partial(interior_kernel, depth=8),
        out_shape=jax.ShapeDtypeStruct((loads, width), F32),
        in_specs=[VMEM, hbm],
        out_specs=VMEM,
        scratch_shapes=[pltpu.VMEM(dirichlet_inv.shape, BF16), pltpu.SemaphoreType.DMA((blocks,))],
        compiler_params=params(),
        cost_estimate=pl.CostEstimate(flops=2 * 16 * blocks * size * size, bytes_accessed=2 * blocks * size * size, transcendentals=0),
        name="interior",
    )(weighted, *pinned(dirichlet_inv))

    face_shape = jax.ShapeDtypeStruct((NF + LANES + rest_rows, LANES), BF16)
    local, send, chosen, near, far = pl.pallas_call(
        level2_kernel,
        out_shape=(
            jax.ShapeDtypeStruct((16, LANES), F32),
            jax.ShapeDtypeStruct((wide, 16, LANES), BF16),
            jax.ShapeDtypeStruct((LANES, LANES), BF16),
            face_shape,
            face_shape,
        ),
        in_specs=[VMEM] * 8,
        out_specs=(VMEM,) * 5,
        scratch_shapes=[pltpu.VMEM((16, LANES), F32), pltpu.VMEM((rest_rows, LANES), F32)],
        compiler_params=params(),
        name="level2",
    )(parts, level2_inv, level2_basis, fine_index, coarse_index, interior, weight, basis)
    near = lax.ppermute(near, "wide", [(i, i ^ 1) for i in range(wide)])
    far = lax.ppermute(far, "wide", [(i, ((i + 1) ^ 1) - 1) for i in range(1, wide - 1)])
    packets = lax.all_to_all(send, "wide", 0, 0)

    send, hot, owner = pl.pallas_call(
        functools.partial(coarse_kernel, width=width),
        out_shape=(
            jax.ShapeDtypeStruct((wide, 16, LANES), BF16),
            jax.ShapeDtypeStruct((LANES, 3 * LANES), BF16),
            jax.ShapeDtypeStruct((8, 3 * LANES), jnp.int32),
        ),
        in_specs=[VMEM] * 3,
        out_specs=(VMEM,) * 3,
        compiler_params=params(),
        name="coarse",
    )(packets, coarse_inv, coarse_index)
    corr = lax.all_to_all(send, "wide", 0, 0)

    return pl.pallas_call(
        tail_kernel,
        out_shape=jax.ShapeDtypeStruct((loads, width), F32),
        in_specs=[VMEM] * 11,
        out_specs=hbm,
        scratch_shapes=[pltpu.VMEM((loads, width), F32), pltpu.SemaphoreType.DMA((4,))],
        compiler_params=params(),
        name="tail",
    )(corr, packets, hot, owner, local, chosen, near, far, interior, inverse, basis)


def solution(mesh):
    placed = (
        P(None, ("wide", "narrow")),
        P(("wide", "narrow")),
        P(("wide", "narrow"), None, None),
        P(("wide", "narrow"), None),
        P(("wide", "narrow"), None),
        P("wide", None),
        P("wide", None),
        P("wide", None),
        P("wide", None),
    )
    return jax.shard_map(
        per_device,
        mesh=mesh,
        in_specs=placed,
        out_specs=P(None, ("wide", "narrow")),
        check_vma=False,
    )
```

```python
import functools

import jax
import jax.numpy as jnp
from jax import lax
from jax.experimental import pallas as pl
from jax.experimental.pallas import tpu as pltpu
from jax.sharding import PartitionSpec as P

NF = 1152
LANES = 128
F32 = jnp.float32
BF16 = jnp.bfloat16
LIMIT = 16 * 1024 * 1024
NN = (((1,), (0,)), ((), ()))
NT = (((1,), (1,)), ((), ()))
VMEM = pl.BlockSpec(memory_space=pltpu.VMEM)


def mm(a, b, dims=NN):
    return lax.dot_general(a, b, dims, preferred_element_type=F32)


def split_mm(a, b, dims=NN):
    high = a.astype(BF16)
    rest = a - high.astype(F32)
    mid = rest.astype(BF16)
    low = (rest - mid.astype(F32)).astype(BF16)
    return mm(high, b, dims) + (mm(mid, b, dims) + mm(low, b, dims))


def selector(index_row, width):
    column = jnp.transpose(jnp.broadcast_to(index_row.astype(F32), (LANES, LANES)))
    lane = lax.broadcasted_iota(jnp.int32, (LANES, LANES), 1).astype(F32)
    return jnp.concatenate(
        [jnp.where(column == lane + float(q * LANES), 1.0, 0.0) for q in range(width // LANES)], axis=1
    ).astype(BF16)


def sides(width):
    me, count = lax.axis_index("wide"), lax.axis_size("wide")
    odd = lax.rem(me, 2)
    last = width - NF
    far = me - 1 + 2 * odd
    inside = jnp.logical_and(far >= 0, far < count)
    return (
        (pl.multiple_of(last * (1 - odd), LANES), me + 1 - 2 * odd, None),
        (pl.multiple_of(last * odd, LANES), jnp.clip(far, 0, count - 1), inside),
    )


def copies_of(pairs, sems):
    copies = [pltpu.make_async_copy(source, target, sems.at[at]) for at, (source, target) in enumerate(pairs)]
    for copy in copies:
        copy.start()
    return copies


def head_kernel(
    resid_hbm,
    mult_hbm,
    basis_hbm,
    index_hbm,
    basis_ref,
    weighted_ref,
    weight_ref,
    inverse_ref,
    send_ref,
    resid_ref,
    mult_ref,
    index_ref,
    sems,
):
    width = resid_ref.shape[1]
    level_width = 4 * LANES
    parts = sems.shape[0] - 3
    step = width // parts
    cuts = [slice(part * step, (part + 1) * step) for part in range(parts)]
    copies = copies_of(
        [(mult_hbm, mult_ref), (resid_hbm, resid_ref), (index_hbm, index_ref)]
        + [(basis_hbm.at[cut], basis_ref.at[cut]) for cut in cuts],
        sems,
    )
    copies[0].wait()
    weight = mult_ref[...].astype(F32)
    weight_ref[...] = weight
    inverse = 1.0 / weight
    inverse_ref[...] = inverse
    copies[1].wait()
    weighted = (resid_ref[...] * inverse).astype(BF16)
    weighted_ref[...] = weighted
    copies[2].wait()
    select = selector(index_ref[...], level_width)
    total = jnp.zeros((resid_ref.shape[0], LANES), F32)
    for part, cut in enumerate(cuts):
        copies[3 + part].wait()
        total += mm(weighted[:, cut], basis_ref[cut, :])
    contrib = split_mm(total, select)
    chunk = jnp.concatenate(
        [contrib[:, q * LANES : (q + 1) * LANES] for q in range(level_width // LANES)], axis=0
    ).astype(BF16)
    for other in range(send_ref.shape[0]):
        send_ref[other] = chunk


def interior_kernel(weighted_ref, blocks_hbm, interior_ref, blocks_ref, sems, *, spans):
    size = blocks_ref.shape[1]
    cuts = [pl.ds(first, blocks) for first, blocks in spans]
    copies = copies_of([(blocks_hbm.at[cut], blocks_ref.at[cut]) for cut in cuts], sems)
    for copy, (first, blocks) in zip(copies, spans):
        copy.wait()
        for b in range(first, first + blocks):
            cut = slice(b * size, (b + 1) * size)
            interior_ref[:, cut] = mm(weighted_ref[:, cut], blocks_ref[b], NT)


def level2_kernel(
    parts_ref,
    inverse_ref,
    level2_basis_ref,
    index_ref,
    coarse_index_ref,
    interior_ref,
    weight_ref,
    basis_ref,
    local_ref,
    send_ref,
    picked_ref,
    near_ref,
    far_ref,
    packet,
    stage,
):
    loads, width = interior_ref.shape
    total = jnp.sum(parts_ref[...].astype(F32), axis=0)
    low = jnp.concatenate([total[q * loads : (q + 1) * loads] for q in range(total.shape[0] // loads)], axis=1).astype(BF16)
    local = mm(low, inverse_ref[...], NT)
    select = selector(index_ref[...], level2_basis_ref.shape[0])
    chosen = mm(select, level2_basis_ref[...]).astype(BF16)
    picked_ref[...] = chosen
    local_picked = split_mm(local, select, NT)
    coarse = coarse_index_ref[...]
    packet[...] = jnp.zeros_like(packet)
    packet[:loads, :] = mm(low, level2_basis_ref[...])
    packet[loads : 2 * loads, :] = local_picked
    packet[8:9, :] = (coarse // LANES).astype(F32)
    packet[9:10, :] = (coarse % LANES).astype(F32)
    local_ref[...] = packet[...]
    chunk = packet[...].astype(BF16)
    for other in range(send_ref.shape[0]):
        send_ref[other] = chunk

    pieces = NF // LANES
    for out_ref, (start, _, _) in zip((near_ref, far_ref), sides(width)):
        out_ref[:NF, :] = basis_ref[pl.ds(start, NF), :]
        out_ref[NF : NF + LANES, :] = chosen
        stage[loads * pieces :, :] = jnp.zeros((stage.shape[0] - loads * pieces, LANES), F32)
        for q in range(pieces):
            lanes = pl.ds(pl.multiple_of(start + q * LANES, LANES), LANES)
            stage[q * loads : (q + 1) * loads, :] = interior_ref[:, lanes]
            stage[loads * pieces + q : loads * pieces + q + 1, :] = weight_ref[:, lanes]
        out_ref[NF + LANES :, :] = stage[...].astype(BF16)


def coarse_kernel(packets_ref, inverse_ref, coarse_index_ref, send_ref, hot_ref, owner_ref, *, width):
    groups = packets_ref.shape[0]
    half = inverse_ref.shape[0]
    highs = inverse_ref.shape[1] // LANES
    row = lax.broadcasted_iota(jnp.int32, (LANES, LANES), 0).astype(F32)
    tall, hot = [], []
    for g in range(groups):
        packet = packets_ref[g].astype(F32)
        values = packet[:8]
        high = jnp.broadcast_to(packet[8:9], (8, LANES))
        tall.append(jnp.concatenate([jnp.where(high == float(h), values, 0.0) for h in range(highs)], axis=0).astype(BF16))
        hot.append(jnp.where(row == jnp.broadcast_to(packet[9:10], (LANES, LANES)), 1.0, 0.0).astype(BF16))
    total = mm(jnp.concatenate(tall, axis=1), jnp.concatenate(hot, axis=1), NT)
    coarse_low = jnp.concatenate([total[8 * h : 8 * h + 8] for h in range(highs)], axis=1).astype(BF16)
    own = mm(coarse_low, inverse_ref[...], NT)
    own = jnp.concatenate([own, jnp.zeros((8, LANES - half), F32)], axis=1)
    chunk = jnp.concatenate([own, jnp.zeros((8, LANES), F32)], axis=0).astype(BF16)
    for other in range(groups):
        send_ref[other] = chunk

    packets = [packets_ref[group].astype(F32) for _, group, _ in sides(width)]
    places = [coarse_index_ref[...].astype(F32)] + [p[8:9] * float(LANES) + p[9:10] for p in packets]
    place = jnp.concatenate(places, axis=1).astype(jnp.int32)
    shape = (LANES, place.shape[1])
    lane = lax.broadcasted_iota(jnp.int32, shape, 0)
    hot_ref[...] = jnp.where(lane == jnp.broadcast_to(place % half, shape), 1.0, 0.0).astype(BF16)
    owner_ref[...] = jnp.broadcast_to(place // half, owner_ref.shape)


def tail_kernel(
    corr_ref,
    packets_ref,
    hot_ref,
    owner_ref,
    local_ref,
    picked_ref,
    near_ref,
    far_ref,
    interior_ref,
    inverse_ref,
    basis_ref,
    out_hbm,
    out_ref,
    sems,
):
    loads, width = interior_ref.shape
    groups = corr_ref.shape[0]
    table = jnp.concatenate([corr_ref[g].astype(F32)[:8] for g in range(groups)], axis=0).astype(BF16)
    picks = mm(table, hot_ref[...])
    owner = owner_ref[...]
    picked = jnp.zeros(owner.shape, F32)
    for g in range(groups):
        picked += jnp.where(owner == g, picks[8 * g : 8 * g + 8], 0.0)
    picked = picked.astype(BF16)
    gathered = (local_ref[4:8, :] + mm(picked[:, :LANES], picked_ref[...], NT)[:loads]).astype(BF16)

    def piece(cut):
        out_ref[:, cut] = (interior_ref[:, cut] + mm(gathered, basis_ref[cut, :], NT)) * inverse_ref[:, cut]

    def send(cut, at):
        copy = pltpu.make_async_copy(out_ref.at[:, cut], out_hbm.at[:, cut], sems.at[at])
        copy.start()
        return copy

    copies = []
    middle = width - 2 * NF
    step = middle // 2
    for at in range(2):
        cut = slice(NF + at * step, NF + (at + 1) * step)
        piece(cut)
        copies.append(send(cut, at))
    ends = [slice(0, NF), slice(width - NF, width)]
    for cut in ends:
        piece(cut)
    pieces = NF // LANES
    for side, (face_ref, (start, group, exists)) in enumerate(zip((near_ref, far_ref), sides(width))):
        lanes = slice((side + 1) * LANES, (side + 2) * LANES)
        packet = packets_ref[group].astype(F32)
        theirs = (packet[4:8] + mm(picked[:, lanes], face_ref[NF : NF + LANES, :], NT)[:loads]).astype(BF16)
        shift = mm(theirs, face_ref[:NF, :], NT)
        rest = face_ref[NF + LANES :, :].astype(F32)
        weight = rest[loads * pieces : loads * pieces + pieces]
        scale = 1.0 / weight
        if exists is not None:
            scale = jnp.where(exists, scale, 0.0)
        for q in range(pieces):
            face = (rest[q * loads : (q + 1) * loads] + shift[:, q * LANES : (q + 1) * LANES]) * scale[q : q + 1]
            at = pl.ds(pl.multiple_of(start + q * LANES, LANES), LANES)
            out_ref[:, at] = out_ref[:, at] + face
    for at, cut in enumerate(ends):
        copies.append(send(cut, 2 + at))
    for copy in copies:
        copy.wait()


def params(limit=LIMIT):
    return pltpu.CompilerParams(vmem_limit_bytes=limit)


def per_device(
    resid,
    mult,
    dirichlet_inv,
    fine_basis,
    fine_index,
    level2_inv,
    level2_basis,
    coarse_index,
    coarse_inv,
):
    loads, width = resid.shape
    blocks, size = dirichlet_inv.shape[0], dirichlet_inv.shape[1]
    wide, narrow = lax.axis_size("wide"), lax.axis_size("narrow")
    mult = mult.reshape(1, width)
    rest_rows = 48

    pieces = 4
    hbm = pl.BlockSpec(memory_space=pltpu.HBM)

    def pinned(*arrays):
        return [pltpu.with_memory_space_constraint(array, pltpu.HBM) for array in arrays]

    basis, weighted, weight, inverse, send = pl.pallas_call(
        head_kernel,
        out_shape=(
            jax.ShapeDtypeStruct(fine_basis.shape, BF16),
            jax.ShapeDtypeStruct((loads, width), BF16),
            jax.ShapeDtypeStruct((1, width), F32),
            jax.ShapeDtypeStruct((1, width), F32),
            jax.ShapeDtypeStruct((narrow, 16, LANES), BF16),
        ),
        in_specs=[hbm] * 4,
        out_specs=(VMEM,) * 5,
        scratch_shapes=[
            pltpu.VMEM(resid.shape, F32),
            pltpu.VMEM(mult.shape, jnp.int32),
            pltpu.VMEM(fine_index.shape, jnp.int32),
            pltpu.SemaphoreType.DMA((3 + pieces,)),
        ],
        compiler_params=params(),
        name="head",
    )(*pinned(resid, mult, fine_basis, fine_index))
    parts = lax.all_to_all(send, "narrow", 0, 0)
    quarter = blocks // 4
    spans = tuple((at, quarter) for at in range(0, blocks, quarter))
    interior = pl.pallas_call(
        functools.partial(interior_kernel, spans=spans),
        out_shape=jax.ShapeDtypeStruct((loads, width), F32),
        in_specs=[VMEM, hbm],
        out_specs=VMEM,
        scratch_shapes=[pltpu.VMEM(dirichlet_inv.shape, BF16), pltpu.SemaphoreType.DMA((len(spans),))],
        compiler_params=params(),
        cost_estimate=pl.CostEstimate(flops=2 * 16 * blocks * size * size, bytes_accessed=2 * blocks * size * size, transcendentals=0),
        name="interior",
    )(weighted, *pinned(dirichlet_inv))

    face_shape = jax.ShapeDtypeStruct((NF + LANES + rest_rows, LANES), BF16)
    local, send, chosen, near, far = pl.pallas_call(
        level2_kernel,
        out_shape=(
            jax.ShapeDtypeStruct((16, LANES), F32),
            jax.ShapeDtypeStruct((wide, 16, LANES), BF16),
            jax.ShapeDtypeStruct((LANES, LANES), BF16),
            face_shape,
            face_shape,
        ),
        in_specs=[VMEM] * 8,
        out_specs=(VMEM,) * 5,
        scratch_shapes=[pltpu.VMEM((16, LANES), F32), pltpu.VMEM((rest_rows, LANES), F32)],
        compiler_params=params(),
        name="level2",
    )(parts, level2_inv, level2_basis, fine_index, coarse_index, interior, weight, basis)
    far = lax.ppermute(far, "wide", [(i, (((i + 1) ^ 1) - 1) % wide) for i in range(wide)])
    near = lax.ppermute(near, "wide", [(i, i ^ 1) for i in range(wide)])
    packets = lax.all_to_all(send, "wide", 0, 0)

    send, hot, owner = pl.pallas_call(
        functools.partial(coarse_kernel, width=width),
        out_shape=(
            jax.ShapeDtypeStruct((wide, 16, LANES), BF16),
            jax.ShapeDtypeStruct((LANES, 3 * LANES), BF16),
            jax.ShapeDtypeStruct((8, 3 * LANES), jnp.int32),
        ),
        in_specs=[VMEM] * 3,
        out_specs=(VMEM,) * 3,
        compiler_params=params(),
        name="coarse",
    )(packets, coarse_inv, coarse_index)
    corr = lax.all_to_all(send, "wide", 0, 0)

    return pl.pallas_call(
        tail_kernel,
        out_shape=jax.ShapeDtypeStruct((loads, width), F32),
        in_specs=[VMEM] * 11,
        out_specs=hbm,
        scratch_shapes=[pltpu.VMEM((loads, width), F32), pltpu.SemaphoreType.DMA((4,))],
        compiler_params=params(),
        name="tail",
    )(corr, packets, hot, owner, local, chosen, near, far, interior, inverse, basis)


def solution(mesh):
    placed = (
        P(None, ("wide", "narrow")),
        P(("wide", "narrow")),
        P(("wide", "narrow"), None, None),
        P(("wide", "narrow"), None),
        P(("wide", "narrow"), None),
        P("wide", None),
        P("wide", None),
        P("wide", None),
        P("wide", None),
    )
    return jax.shard_map(
        per_device,
        mesh=mesh,
        in_specs=placed,
        out_specs=P(None, ("wide", "narrow")),
        check_vma=False,
    )
```

```python
import functools

import jax
import jax.numpy as jnp
from jax import lax
from jax.experimental import pallas as pl
from jax.experimental.pallas import tpu as pltpu
from jax.sharding import PartitionSpec as P

NF = 1152
LANES = 128
REST = 64
LOCAL = 48
F32 = jnp.float32
BF16 = jnp.bfloat16
LIMIT = 16 * 1024 * 1024
NN = (((1,), (0,)), ((), ()))
NT = (((1,), (1,)), ((), ()))
VMEM = pl.BlockSpec(memory_space=pltpu.VMEM)


def mm(a, b, dims=NN):
    return lax.dot_general(a, b, dims, preferred_element_type=F32)


def split_mm(a, b, dims=NN):
    high = a.astype(BF16)
    rest = a - high.astype(F32)
    mid = rest.astype(BF16)
    low = (rest - mid.astype(F32)).astype(BF16)
    return mm(high, b, dims) + (mm(mid, b, dims) + mm(low, b, dims))


def side_by_side(a, b):
    zero = jnp.zeros_like(a)
    return jnp.concatenate([jnp.concatenate([a, zero], axis=1), jnp.concatenate([zero, b], axis=1)], axis=0).astype(BF16)


def selector(index_row, width):
    column = jnp.transpose(jnp.broadcast_to(index_row.astype(F32), (LANES, LANES)))
    lane = lax.broadcasted_iota(jnp.int32, (LANES, LANES), 1).astype(F32)
    return jnp.concatenate(
        [jnp.where(column == lane + float(q * LANES), 1.0, 0.0) for q in range(width // LANES)], axis=1
    ).astype(BF16)


def sides(width):
    me, count = lax.axis_index("wide"), lax.axis_size("wide")
    odd = lax.rem(me, 2)
    last = width - NF
    far = me - 1 + 2 * odd
    inside = jnp.logical_and(far >= 0, far < count)
    return (
        (pl.multiple_of(last * (1 - odd), LANES), me + 1 - 2 * odd, None),
        (pl.multiple_of(last * odd, LANES), jnp.clip(far, 0, count - 1), inside),
    )


def copies_of(pairs, sems):
    copies = [pltpu.make_async_copy(source, target, sems.at[at]) for at, (source, target) in enumerate(pairs)]
    for copy in copies:
        copy.start()
    return copies


def head_kernel(
    resid_hbm,
    mult_hbm,
    basis_hbm,
    index_hbm,
    basis_ref,
    weighted_ref,
    inverse_ref,
    send_ref,
    resid_ref,
    mult_ref,
    index_ref,
    sems,
):
    width = resid_ref.shape[1]
    level_width = 4 * LANES
    loads = resid_ref.shape[0]
    parts = sems.shape[0] - 3
    step = width // parts
    cuts = [slice(part * step, (part + 1) * step) for part in range(parts)]
    copies = copies_of(
        [(mult_hbm, mult_ref), (resid_hbm, resid_ref), (index_hbm, index_ref)]
        + [(basis_hbm.at[cut], basis_ref.at[cut]) for cut in cuts],
        sems,
    )
    copies[0].wait()
    inverse = 1.0 / mult_ref[...].astype(F32)
    inverse_ref[...] = inverse
    copies[1].wait()
    weighted = resid_ref[...] * inverse
    weighted_ref[...] = weighted.astype(BF16)
    copies[2].wait()
    select = selector(index_ref[...], level_width)
    total = jnp.zeros((2 * loads, 2 * LANES), F32)
    for part, cut in enumerate(cuts):
        copies[3 + part].wait()
        first, second = slice(cut.start, cut.start + step // 2), slice(cut.start + step // 2, cut.stop)
        total += mm(
            jnp.concatenate([weighted[:, first], weighted[:, second]], axis=0).astype(BF16),
            jnp.concatenate([basis_ref[first, :], basis_ref[second, :]], axis=1),
        )
    total = total[:loads, :LANES] + total[loads:, LANES:]
    contrib = split_mm(total, select)
    chunk = jnp.concatenate(
        [contrib[:, q * LANES : (q + 1) * LANES] for q in range(level_width // LANES)], axis=0
    ).astype(BF16)
    for other in range(send_ref.shape[0]):
        send_ref[other] = chunk


def interior_kernel(weighted_ref, blocks_hbm, coarse_inv_hbm, interior_ref, tiles_ref, blocks_ref, sems, *, spans):
    size = blocks_ref.shape[1]
    whole = size // 256 * 256
    cuts = [pl.ds(first, blocks) for first, blocks in spans]
    pairs = [(blocks_hbm.at[cut], blocks_ref.at[cut]) for cut in cuts]
    pairs += [(coarse_inv_hbm.at[:, pl.ds(h * LANES, LANES)], tiles_ref.at[h]) for h in range(tiles_ref.shape[0])]
    copies = copies_of(pairs, sems)
    for copy, (first, blocks) in zip(copies, spans):
        copy.wait()
        for b in range(first, first + blocks, 2):
            one, two = slice(b * size, (b + 1) * size), slice((b + 1) * size, (b + 2) * size)
            left, right = weighted_ref[:, one].astype(F32), weighted_ref[:, two].astype(F32)
            rest = mm(
                side_by_side(left[:, whole:], right[:, whole:]),
                jnp.concatenate([blocks_ref[b][:, whole:], blocks_ref[b + 1][:, whole:]], axis=1),
                NT,
            )
            loads = left.shape[0]
            first_sum = mm(left[:, :whole].astype(BF16), blocks_ref[b][:, :whole], NT) + rest[:loads]
            second_sum = mm(right[:, :whole].astype(BF16), blocks_ref[b + 1][:, :whole], NT) + rest[loads:]
            interior_ref[:, one] = first_sum.astype(BF16)
            interior_ref[:, two] = second_sum.astype(BF16)
    for copy in copies[len(spans) :]:
        copy.wait()


def level2_kernel(
    parts_ref,
    inverse_ref,
    level2_basis_ref,
    index_ref,
    coarse_index_ref,
    interior_ref,
    inverse_mult_ref,
    basis_ref,
    tiles_ref,
    local_ref,
    send_ref,
    picked_ref,
    near_ref,
    far_ref,
    packet,
    stage,
):
    loads, width = interior_ref.shape
    rows = stage.shape[0]
    total = jnp.sum(parts_ref[...].astype(F32), axis=0)
    low = jnp.concatenate([total[q * loads : (q + 1) * loads] for q in range(total.shape[0] // loads)], axis=1).astype(BF16)
    local = mm(low, inverse_ref[...], NT)
    select = selector(index_ref[...], level2_basis_ref.shape[0])
    chosen = mm(select, level2_basis_ref[...]).astype(BF16)
    picked_ref[...] = chosen
    local_picked = split_mm(local, select, NT)
    local_ref[...] = local_picked
    coarse = coarse_index_ref[...]
    packet[:loads, :] = mm(low, level2_basis_ref[...])
    packet[loads : loads + 1, :] = (coarse // LANES).astype(F32)
    packet[loads + 1 : loads + 2, :] = (coarse % LANES).astype(F32)
    packet[loads + 2 :, :] = jnp.zeros((packet.shape[0] - loads - 2, LANES), F32)
    chunk = packet[...].astype(BF16)
    for other in range(send_ref.shape[0]):
        send_ref[other] = chunk

    pieces = NF // LANES
    for out_ref, (start, _, _) in zip((near_ref, far_ref), sides(width)):
        out_ref[:NF, :] = basis_ref[pl.ds(start, NF), :]
        out_ref[NF : NF + LANES, :] = chosen
        stage[loads * pieces :, :] = jnp.zeros((rows - loads * pieces, LANES), F32)
        for q in range(pieces):
            lanes = pl.ds(pl.multiple_of(start + q * LANES, LANES), LANES)
            stage[q * loads : (q + 1) * loads, :] = interior_ref[:, lanes].astype(F32)
            stage[loads * pieces + q : loads * pieces + q + 1, :] = jnp.round(1.0 / inverse_mult_ref[:, lanes])
        stage[LOCAL : LOCAL + loads, :] = local_picked
        out_ref[NF + LANES : NF + LANES + rows, :] = stage[...].astype(BF16)
    count = tiles_ref.shape[1]
    for h in range(tiles_ref.shape[0]):
        at = NF + LANES + rows + h * count
        near_ref[at : at + count, :] = tiles_ref[h]


def coarse_kernel(packets_ref, tiles_ref, coarse_index_ref, near_ref, send_ref, hot_ref, owner_ref, *, width):
    loads = 4
    groups, rows = packets_ref.shape[0], packets_ref.shape[1]
    highs, count = tiles_ref.shape[0], tiles_ref.shape[1]
    row = lax.broadcasted_iota(jnp.int32, (LANES, LANES), 0).astype(F32)
    tall, hot = [], []
    for g in range(groups):
        packet = packets_ref[g].astype(F32)
        high = jnp.broadcast_to(packet[loads : loads + 1], (rows, LANES))
        low = jnp.broadcast_to(packet[loads + 1 : loads + 2], (LANES, LANES))
        tall.append(jnp.concatenate([jnp.where(high == float(h), packet, 0.0) for h in range(highs)], axis=0).astype(BF16))
        hot.append(jnp.where(row == low, 1.0, 0.0).astype(BF16))
    total = mm(jnp.concatenate(tall, axis=1), jnp.concatenate(hot, axis=1), NT)
    coarse_low = jnp.concatenate([total[rows * h : rows * (h + 1)] for h in range(highs)], axis=1).astype(BF16)
    own = mm(coarse_low, jnp.concatenate([tiles_ref[h] for h in range(highs)], axis=1), NT)
    first = near_ref.shape[0] - highs * count
    theirs = jnp.concatenate([near_ref[first + h * count : first + (h + 1) * count, :] for h in range(highs)], axis=1)
    other = mm(coarse_low, theirs, NT)
    odd = lax.rem(lax.axis_index("wide"), 2) == 1
    chunk = jnp.concatenate([jnp.where(odd, other, own), jnp.where(odd, own, other)], axis=1).astype(BF16)
    for at in range(send_ref.shape[0]):
        send_ref[at] = chunk

    packets = [packets_ref[group].astype(F32) for _, group, _ in sides(width)]
    coarse = coarse_index_ref[...]
    owner = jnp.concatenate([(coarse // LANES).astype(F32)] + [p[loads : loads + 1] for p in packets], axis=1)
    within = jnp.concatenate([(coarse % LANES).astype(F32)] + [p[loads + 1 : loads + 2] for p in packets], axis=1)
    shape = (LANES, within.shape[1])
    lane = lax.broadcasted_iota(jnp.int32, shape, 0).astype(F32)
    hot_ref[...] = jnp.where(lane == jnp.broadcast_to(within, shape), 1.0, 0.0).astype(BF16)
    owner_ref[...] = jnp.broadcast_to(owner, owner_ref.shape)


def tail_kernel(
    corr_ref,
    hot_ref,
    owner_ref,
    local_ref,
    picked_ref,
    near_ref,
    far_ref,
    interior_ref,
    inverse_ref,
    basis_ref,
    out_hbm,
    out_ref,
    sems,
):
    loads, width = interior_ref.shape
    half = width // 2
    pieces = NF // LANES
    chips, rows = corr_ref.shape[0], corr_ref.shape[1]
    table = jnp.concatenate([corr_ref[c].astype(F32) for c in range(chips)], axis=0).astype(BF16)
    picks = mm(table, hot_ref[...])
    owner = owner_ref[...]
    picked = jnp.zeros(owner.shape, F32)
    for c in range(chips):
        picked += jnp.where(owner == float(c), picks[rows * c : rows * (c + 1)], 0.0)
    picked = picked.astype(BF16)
    gathered = local_ref[...] + mm(picked[:, :LANES], picked_ref[...], NT)[:loads]
    gathered = side_by_side(gathered, gathered)
    theirs, rests = [], []
    for side, face_ref in enumerate((near_ref, far_ref)):
        lanes = slice((side + 1) * LANES, (side + 2) * LANES)
        rest = face_ref[NF + LANES : NF + LANES + REST, :].astype(F32)
        theirs.append(rest[LOCAL : LOCAL + loads] + mm(picked[:, lanes], face_ref[NF : NF + LANES, :], NT)[:loads])
        rests.append(rest)
    shifts = mm(side_by_side(*theirs), jnp.concatenate([near_ref[:NF, :], far_ref[:NF, :]], axis=1), NT)

    copies = []

    def piece(at, count):
        one, two = slice(at, at + count), slice(half + at, half + at + count)
        shift = mm(gathered, jnp.concatenate([basis_ref[one, :], basis_ref[two, :]], axis=1), NT)
        out_ref[:, one] = (interior_ref[:, one].astype(F32) + shift[:loads]) * inverse_ref[:, one]
        out_ref[:, two] = (interior_ref[:, two].astype(F32) + shift[loads:]) * inverse_ref[:, two]
        return one, two

    def send(cut):
        copy = pltpu.make_async_copy(out_ref.at[:, cut], out_hbm.at[:, cut], sems.at[len(copies)])
        copy.start()
        copies.append(copy)

    cuts = piece(0, half // 2) + piece(half // 2, half // 2)
    send(cuts[1])
    send(cuts[2])
    for side, (start, _, exists) in enumerate(sides(width)):
        rest, shift = rests[side], shifts[side * loads : (side + 1) * loads]
        scale = 1.0 / rest[loads * pieces : loads * pieces + pieces]
        if exists is not None:
            scale = jnp.where(exists, scale, 0.0)
        for q in range(pieces):
            face = (rest[q * loads : (q + 1) * loads] + shift[:, q * LANES : (q + 1) * LANES]) * scale[q : q + 1]
            at = pl.ds(pl.multiple_of(start + q * LANES, LANES), LANES)
            out_ref[:, at] = out_ref[:, at] + face
    send(cuts[0])
    send(cuts[3])
    for copy in copies:
        copy.wait()


def params(limit=LIMIT):
    return pltpu.CompilerParams(vmem_limit_bytes=limit)


def per_device(
    resid,
    mult,
    dirichlet_inv,
    fine_basis,
    fine_index,
    level2_inv,
    level2_basis,
    coarse_index,
    coarse_inv,
):
    loads, width = resid.shape
    blocks, size = dirichlet_inv.shape[0], dirichlet_inv.shape[1]
    wide, narrow = lax.axis_size("wide"), lax.axis_size("narrow")
    mult = mult.reshape(1, width)

    pieces = 4
    hbm = pl.BlockSpec(memory_space=pltpu.HBM)

    def pinned(*arrays):
        return [pltpu.with_memory_space_constraint(array, pltpu.HBM) for array in arrays]

    basis, weighted, inverse, send = pl.pallas_call(
        head_kernel,
        out_shape=(
            jax.ShapeDtypeStruct(fine_basis.shape, BF16),
            jax.ShapeDtypeStruct((loads, width), BF16),
            jax.ShapeDtypeStruct((1, width), F32),
            jax.ShapeDtypeStruct((narrow, 16, LANES), BF16),
        ),
        in_specs=[hbm] * 4,
        out_specs=(VMEM,) * 4,
        scratch_shapes=[
            pltpu.VMEM(resid.shape, F32),
            pltpu.VMEM(mult.shape, jnp.int32),
            pltpu.VMEM(fine_index.shape, jnp.int32),
            pltpu.SemaphoreType.DMA((3 + pieces,)),
        ],
        compiler_params=params(),
        name="head",
    )(*pinned(resid, mult, fine_basis, fine_index))
    parts = lax.all_to_all(send, "narrow", 0, 0)
    sixth = blocks // 6
    spans = tuple((at, sixth) for at in range(0, blocks, sixth))
    highs = coarse_inv.shape[1] // LANES
    interior, tiles = pl.pallas_call(
        functools.partial(interior_kernel, spans=spans),
        out_shape=(
            jax.ShapeDtypeStruct((loads, width), BF16),
            jax.ShapeDtypeStruct((highs, coarse_inv.shape[0], LANES), BF16),
        ),
        input_output_aliases={0: 0},
        in_specs=[VMEM, hbm, hbm],
        out_specs=(VMEM, VMEM),
        scratch_shapes=[pltpu.VMEM(dirichlet_inv.shape, BF16), pltpu.SemaphoreType.DMA((len(spans) + highs,))],
        compiler_params=params(),
        cost_estimate=pl.CostEstimate(flops=2 * 16 * blocks * size * size, bytes_accessed=2 * blocks * size * size, transcendentals=0),
        name="interior",
    )(weighted, *pinned(dirichlet_inv, coarse_inv))

    near_rows = NF + LANES + REST + coarse_inv.size // LANES
    local, send, chosen, near, far = pl.pallas_call(
        level2_kernel,
        out_shape=(
            jax.ShapeDtypeStruct((loads, LANES), F32),
            jax.ShapeDtypeStruct((wide, 8, LANES), BF16),
            jax.ShapeDtypeStruct((LANES, LANES), BF16),
            jax.ShapeDtypeStruct((near_rows, LANES), BF16),
            jax.ShapeDtypeStruct((NF + LANES + REST, LANES), BF16),
        ),
        in_specs=[VMEM] * 9,
        out_specs=(VMEM,) * 5,
        scratch_shapes=[
            pltpu.VMEM((8, LANES), F32),
            pltpu.VMEM((REST, LANES), F32),
        ],
        compiler_params=params(),
        name="level2",
    )(parts, level2_inv, level2_basis, fine_index, coarse_index, interior, inverse, basis, tiles)
    far = lax.ppermute(far, "wide", [(i, (((i + 1) ^ 1) - 1) % wide) for i in range(wide)])
    near = lax.ppermute(near, "wide", [(i, i ^ 1) for i in range(wide)])
    packets = lax.all_to_all(send, "wide", 0, 0)

    send, hot, owner = pl.pallas_call(
        functools.partial(coarse_kernel, width=width),
        out_shape=(
            jax.ShapeDtypeStruct((wide // 2, 8, LANES), BF16),
            jax.ShapeDtypeStruct((LANES, 3 * LANES), BF16),
            jax.ShapeDtypeStruct((8, 3 * LANES), F32),
        ),
        in_specs=[VMEM] * 4,
        out_specs=(VMEM,) * 3,
        compiler_params=params(),
        name="coarse",
    )(packets, tiles, coarse_index, near)
    send, near, far = lax.optimization_barrier((send, near, far))
    cores = [[chip * 2 + core for chip in range(wide // 2)] for core in range(2)]
    corr = lax.all_to_all(send, "wide", 0, 0, axis_index_groups=cores)

    return pl.pallas_call(
        tail_kernel,
        out_shape=jax.ShapeDtypeStruct((loads, width), F32),
        in_specs=[VMEM] * 10,
        out_specs=hbm,
        scratch_shapes=[pltpu.VMEM((loads, width), F32), pltpu.SemaphoreType.DMA((4,))],
        compiler_params=params(),
        name="tail",
    )(corr, hot, owner, local, chosen, near, far, interior, inverse, basis)


def solution(mesh):
    placed = (
        P(None, ("wide", "narrow")),
        P(("wide", "narrow")),
        P(("wide", "narrow"), None, None),
        P(("wide", "narrow"), None),
        P(("wide", "narrow"), None),
        P("wide", None),
        P("wide", None),
        P("wide", None),
        P("wide", None),
    )
    return jax.shard_map(
        per_device,
        mesh=mesh,
        in_specs=placed,
        out_specs=P(None, ("wide", "narrow")),
        check_vma=False,
    )
```

```python
import functools

import jax
import jax.numpy as jnp
from jax import lax
from jax.experimental import pallas as pl
from jax.experimental.pallas import tpu as pltpu
from jax.sharding import PartitionSpec as P

NF = 1152
LANES = 128
REST = 64
LOCAL = 48
F32 = jnp.float32
BF16 = jnp.bfloat16
LIMIT = 16 * 1024 * 1024
NN = (((1,), (0,)), ((), ()))
NT = (((1,), (1,)), ((), ()))
VMEM = pl.BlockSpec(memory_space=pltpu.VMEM)


def mm(a, b, dims=NN):
    return lax.dot_general(a, b, dims, preferred_element_type=F32)


def split_mm(a, b, dims=NN):
    high = a.astype(BF16)
    rest = a - high.astype(F32)
    mid = rest.astype(BF16)
    low = (rest - mid.astype(F32)).astype(BF16)
    return mm(high, b, dims) + (mm(mid, b, dims) + mm(low, b, dims))


def side_by_side(a, b):
    zero = jnp.zeros_like(a)
    return jnp.concatenate([jnp.concatenate([a, zero], axis=1), jnp.concatenate([zero, b], axis=1)], axis=0).astype(BF16)


def selector(index_row, width):
    column = jnp.transpose(jnp.broadcast_to(index_row.astype(F32), (LANES, LANES)))
    lane = lax.broadcasted_iota(jnp.int32, (LANES, LANES), 1).astype(F32)
    return jnp.concatenate(
        [jnp.where(column == lane + float(q * LANES), 1.0, 0.0) for q in range(width // LANES)], axis=1
    ).astype(BF16)


def sides(width):
    me, count = lax.axis_index("wide"), lax.axis_size("wide")
    odd = lax.rem(me, 2)
    last = width - NF
    far = me - 1 + 2 * odd
    inside = jnp.logical_and(far >= 0, far < count)
    return (
        (pl.multiple_of(last * (1 - odd), LANES), me + 1 - 2 * odd, None),
        (pl.multiple_of(last * odd, LANES), jnp.clip(far, 0, count - 1), inside),
    )


def copies_of(pairs, sems):
    copies = [pltpu.make_async_copy(source, target, sems.at[at]) for at, (source, target) in enumerate(pairs)]
    for copy in copies:
        copy.start()
    return copies


def head_kernel(
    resid_hbm,
    mult_hbm,
    basis_hbm,
    index_hbm,
    basis_ref,
    weighted_ref,
    inverse_ref,
    send_ref,
    resid_ref,
    mult_ref,
    index_ref,
    sems,
):
    width = resid_ref.shape[1]
    level_width = 4 * LANES
    loads = resid_ref.shape[0]
    parts = sems.shape[0] - 3
    step = width // parts
    cuts = [slice(part * step, (part + 1) * step) for part in range(parts)]
    copies = copies_of(
        [(mult_hbm, mult_ref), (resid_hbm, resid_ref), (index_hbm, index_ref)]
        + [(basis_hbm.at[cut], basis_ref.at[cut]) for cut in cuts],
        sems,
    )
    copies[0].wait()
    inverse = 1.0 / mult_ref[...].astype(F32)
    inverse_ref[...] = inverse
    copies[1].wait()
    weighted = resid_ref[...] * inverse
    weighted_ref[...] = weighted.astype(BF16)
    copies[2].wait()
    select = selector(index_ref[...], level_width)
    total = jnp.zeros((2 * loads, 2 * LANES), F32)
    for part, cut in enumerate(cuts):
        copies[3 + part].wait()
        first, second = slice(cut.start, cut.start + step // 2), slice(cut.start + step // 2, cut.stop)
        total += mm(
            jnp.concatenate([weighted[:, first], weighted[:, second]], axis=0).astype(BF16),
            jnp.concatenate([basis_ref[first, :], basis_ref[second, :]], axis=1),
        )
    total = total[:loads, :LANES] + total[loads:, LANES:]
    contrib = split_mm(total, select)
    chunk = jnp.concatenate(
        [contrib[:, q * LANES : (q + 1) * LANES] for q in range(level_width // LANES)], axis=0
    ).astype(BF16)
    for other in range(send_ref.shape[0]):
        send_ref[other] = chunk


def interior_kernel(weighted_ref, blocks_hbm, coarse_inv_hbm, interior_ref, tiles_ref, blocks_ref, rows_ref, sems, *, spans):
    size = blocks_ref.shape[1]
    whole = size // 256 * 256
    cuts = [pl.ds(first, blocks) for first, blocks in spans]
    copies = copies_of([(coarse_inv_hbm, rows_ref)] + [(blocks_hbm.at[cut], blocks_ref.at[cut]) for cut in cuts], sems)
    copies[0].wait()
    for p in range(tiles_ref.shape[0]):
        rows = [rows_ref[:, (2 * p + i) * LANES : (2 * p + i + 1) * LANES].astype(F32) for i in range(2)]
        tiles_ref[p] = jnp.transpose(jnp.concatenate(rows, axis=0)).astype(BF16)
    for copy, (first, blocks) in zip(copies[1:], spans):
        copy.wait()
        for b in range(first, first + blocks, 2):
            one, two = slice(b * size, (b + 1) * size), slice((b + 1) * size, (b + 2) * size)
            left, right = weighted_ref[:, one].astype(F32), weighted_ref[:, two].astype(F32)
            rest = mm(
                side_by_side(left[:, whole:], right[:, whole:]),
                jnp.concatenate([blocks_ref[b][:, whole:], blocks_ref[b + 1][:, whole:]], axis=1),
                NT,
            )
            loads = left.shape[0]
            first_sum = mm(left[:, :whole].astype(BF16), blocks_ref[b][:, :whole], NT) + rest[:loads]
            second_sum = mm(right[:, :whole].astype(BF16), blocks_ref[b + 1][:, :whole], NT) + rest[loads:]
            interior_ref[:, one] = first_sum.astype(BF16)
            interior_ref[:, two] = second_sum.astype(BF16)


def level2_kernel(
    parts_ref,
    inverse_ref,
    level2_basis_ref,
    index_ref,
    coarse_index_ref,
    interior_ref,
    inverse_mult_ref,
    basis_ref,
    tiles_ref,
    local_ref,
    send_ref,
    picked_ref,
    near_ref,
    far_ref,
    packet,
    stage,
):
    loads, width = interior_ref.shape
    rows = stage.shape[0]
    total = jnp.sum(parts_ref[...].astype(F32), axis=0)
    low = jnp.concatenate([total[q * loads : (q + 1) * loads] for q in range(total.shape[0] // loads)], axis=1).astype(BF16)
    local = mm(low, inverse_ref[...], NT)
    select = selector(index_ref[...], level2_basis_ref.shape[0])
    chosen = mm(select, level2_basis_ref[...]).astype(BF16)
    picked_ref[...] = chosen
    local_picked = split_mm(local, select, NT)
    local_ref[...] = local_picked
    coarse = coarse_index_ref[...]
    packet[:loads, :] = mm(low, level2_basis_ref[...])
    packet[loads : loads + 1, :] = (coarse // LANES).astype(F32)
    packet[loads + 1 : loads + 2, :] = (coarse % LANES).astype(F32)
    packet[loads + 2 :, :] = jnp.zeros((packet.shape[0] - loads - 2, LANES), F32)
    chunk = packet[...].astype(BF16)
    for other in range(send_ref.shape[0]):
        send_ref[other] = chunk

    pieces = NF // LANES
    for out_ref, (start, _, _) in zip((near_ref, far_ref), sides(width)):
        out_ref[:NF, :] = basis_ref[pl.ds(start, NF), :]
        out_ref[NF : NF + LANES, :] = chosen
        stage[loads * pieces :, :] = jnp.zeros((rows - loads * pieces, LANES), F32)
        for q in range(pieces):
            lanes = pl.ds(pl.multiple_of(start + q * LANES, LANES), LANES)
            stage[q * loads : (q + 1) * loads, :] = interior_ref[:, lanes].astype(F32)
            stage[loads * pieces + q : loads * pieces + q + 1, :] = jnp.round(1.0 / inverse_mult_ref[:, lanes])
        stage[LOCAL : LOCAL + loads, :] = local_picked
        out_ref[NF + LANES : NF + LANES + rows, :] = stage[...].astype(BF16)
    count = tiles_ref.shape[1]
    for h in range(tiles_ref.shape[0]):
        at = NF + LANES + rows + h * count
        near_ref[at : at + count, :] = tiles_ref[h]


def coarse_kernel(packets_ref, tiles_ref, coarse_index_ref, near_ref, send_ref, hot_ref, owner_ref, *, width):
    loads = 4
    groups, rows = packets_ref.shape[0], packets_ref.shape[1]
    pairs = tiles_ref.shape[0]
    highs, count = 2 * pairs, tiles_ref.shape[2] // 2
    row = lax.broadcasted_iota(jnp.int32, (LANES, LANES), 0).astype(F32).astype(BF16)
    tall, hot = [], []
    for g in range(groups):
        packet = packets_ref[g].astype(F32)
        twice = jnp.concatenate([packet, packet], axis=0).astype(BF16)
        high = jnp.broadcast_to(packet[loads : loads + 1], (2 * rows, LANES))
        which = jnp.concatenate([jnp.zeros((rows, LANES), F32), jnp.ones((rows, LANES), F32)], axis=0)
        high = (high - which).astype(BF16)
        low = jnp.broadcast_to(packet[loads + 1 : loads + 2], (LANES, LANES)).astype(BF16)
        zero, one = jnp.zeros((), BF16), jnp.ones((), BF16)
        tall.append(jnp.concatenate([jnp.where(high == jnp.asarray(h, BF16), twice, zero) for h in range(0, highs, 2)], axis=0))
        hot.append(jnp.where(row == low, one, zero))
    total = mm(jnp.concatenate(tall, axis=1), jnp.concatenate(hot, axis=1), NT)
    coarse_low = jnp.concatenate(
        [jnp.concatenate([total[rows * h : rows * (h + 1)] for h in range(i, highs, 2)], axis=1) for i in range(2)], axis=0
    ).astype(BF16)
    tiles = jnp.concatenate([tiles_ref[p] for p in range(pairs)], axis=0)
    theirs = near_ref[near_ref.shape[0] - pairs * LANES :, :]
    both = mm(coarse_low, jnp.concatenate([tiles, theirs], axis=1))
    own = both[:rows, :count] + both[rows:, count : 2 * count]
    other = both[:rows, 2 * count : 3 * count] + both[rows:, 3 * count :]
    odd = lax.rem(lax.axis_index("wide"), 2) == 1
    chunk = jnp.concatenate([jnp.where(odd, other, own), jnp.where(odd, own, other)], axis=1).astype(BF16)
    for at in range(send_ref.shape[0]):
        send_ref[at] = chunk

    packets = [packets_ref[group].astype(F32) for _, group, _ in sides(width)]
    coarse = coarse_index_ref[...]
    owner = jnp.concatenate([(coarse // LANES).astype(F32)] + [p[loads : loads + 1] for p in packets], axis=1)
    within = jnp.concatenate([(coarse % LANES).astype(F32)] + [p[loads + 1 : loads + 2] for p in packets], axis=1)
    shape = (LANES, within.shape[1])
    lane = lax.broadcasted_iota(jnp.int32, shape, 0).astype(F32)
    hot_ref[...] = jnp.where(lane == jnp.broadcast_to(within, shape), 1.0, 0.0).astype(BF16)
    owner_ref[...] = jnp.broadcast_to(owner, owner_ref.shape)


def tail_kernel(
    corr_ref,
    hot_ref,
    owner_ref,
    local_ref,
    picked_ref,
    near_ref,
    far_ref,
    interior_ref,
    inverse_ref,
    basis_ref,
    out_hbm,
    out_ref,
    sems,
):
    loads, width = interior_ref.shape
    half = width // 2
    pieces = NF // LANES
    chips, rows = corr_ref.shape[0], corr_ref.shape[1]
    table = jnp.concatenate([corr_ref[c].astype(F32) for c in range(chips)], axis=0).astype(BF16)
    picks = mm(table, hot_ref[...])
    owner = owner_ref[...]
    picked = jnp.zeros(owner.shape, F32)
    for c in range(chips):
        picked += jnp.where(owner == float(c), picks[rows * c : rows * (c + 1)], 0.0)
    picked = picked.astype(BF16)
    gathered = local_ref[...] + mm(picked[:, :LANES], picked_ref[...], NT)[:loads]
    gathered = side_by_side(gathered, gathered)
    theirs, rests = [], []
    for side, face_ref in enumerate((near_ref, far_ref)):
        lanes = slice((side + 1) * LANES, (side + 2) * LANES)
        rest = face_ref[NF + LANES : NF + LANES + REST, :].astype(F32)
        theirs.append(rest[LOCAL : LOCAL + loads] + mm(picked[:, lanes], face_ref[NF : NF + LANES, :], NT)[:loads])
        rests.append(rest)
    shifts = mm(side_by_side(*theirs), jnp.concatenate([near_ref[:NF, :], far_ref[:NF, :]], axis=1), NT)

    copies = []

    def piece(at, count):
        one, two = slice(at, at + count), slice(half + at, half + at + count)
        shift = mm(gathered, jnp.concatenate([basis_ref[one, :], basis_ref[two, :]], axis=1), NT)
        out_ref[:, one] = (interior_ref[:, one].astype(F32) + shift[:loads]) * inverse_ref[:, one]
        out_ref[:, two] = (interior_ref[:, two].astype(F32) + shift[loads:]) * inverse_ref[:, two]
        return one, two

    def send(cut):
        copy = pltpu.make_async_copy(out_ref.at[:, cut], out_hbm.at[:, cut], sems.at[len(copies)])
        copy.start()
        copies.append(copy)

    faces = []
    for side, (_, _, exists) in enumerate(sides(width)):
        rest, shift = rests[side], shifts[side * loads : (side + 1) * loads]
        weights = jnp.concatenate([rest[loads * pieces + q : loads * pieces + q + 1] for q in range(pieces)], axis=1)
        scale = 1.0 / weights
        if exists is not None:
            scale = jnp.where(exists, scale, 0.0)
        inside = jnp.concatenate([rest[q * loads : (q + 1) * loads] for q in range(pieces)], axis=1)
        faces.append((inside + shift) * scale)
    odd = lax.rem(lax.axis_index("wide"), 2) == 1
    from_below, from_above = jnp.where(odd, faces[0], faces[1]), jnp.where(odd, faces[1], faces[0])

    one, two = piece(0, half // 2)
    out_ref[:, :NF] = out_ref[:, :NF] + from_below
    send(one)
    send(two)
    one, two = piece(half // 2, half // 2)
    send(one)
    out_ref[:, width - NF :] = out_ref[:, width - NF :] + from_above
    send(two)
    for copy in copies:
        copy.wait()


def params(limit=LIMIT):
    return pltpu.CompilerParams(vmem_limit_bytes=limit)


def per_device(
    resid,
    mult,
    dirichlet_inv,
    fine_basis,
    fine_index,
    level2_inv,
    level2_basis,
    coarse_index,
    coarse_inv,
):
    loads, width = resid.shape
    blocks, size = dirichlet_inv.shape[0], dirichlet_inv.shape[1]
    wide, narrow = lax.axis_size("wide"), lax.axis_size("narrow")
    mult = mult.reshape(1, width)

    pieces = 3
    hbm = pl.BlockSpec(memory_space=pltpu.HBM)

    def pinned(*arrays):
        return [pltpu.with_memory_space_constraint(array, pltpu.HBM) for array in arrays]

    basis, weighted, inverse, send = pl.pallas_call(
        head_kernel,
        out_shape=(
            jax.ShapeDtypeStruct(fine_basis.shape, BF16),
            jax.ShapeDtypeStruct((loads, width), BF16),
            jax.ShapeDtypeStruct((1, width), F32),
            jax.ShapeDtypeStruct((narrow, 16, LANES), BF16),
        ),
        in_specs=[hbm] * 4,
        out_specs=(VMEM,) * 4,
        scratch_shapes=[
            pltpu.VMEM(resid.shape, F32),
            pltpu.VMEM(mult.shape, jnp.int32),
            pltpu.VMEM(fine_index.shape, jnp.int32),
            pltpu.SemaphoreType.DMA((3 + pieces,)),
        ],
        compiler_params=params(),
        name="head",
    )(*pinned(resid, mult, fine_basis, fine_index))
    parts = lax.all_to_all(send, "narrow", 0, 0)
    sixth = blocks // 6
    spans = tuple((at, sixth) for at in range(0, blocks, sixth))
    highs = coarse_inv.shape[1] // LANES
    interior, tiles = pl.pallas_call(
        functools.partial(interior_kernel, spans=spans),
        out_shape=(
            jax.ShapeDtypeStruct((loads, width), BF16),
            jax.ShapeDtypeStruct((highs // 2, LANES, LANES), BF16),
        ),
        input_output_aliases={0: 0},
        in_specs=[VMEM, hbm, hbm],
        out_specs=(VMEM, VMEM),
        scratch_shapes=[
            pltpu.VMEM(dirichlet_inv.shape, BF16),
            pltpu.VMEM(coarse_inv.shape, BF16),
            pltpu.SemaphoreType.DMA((len(spans) + 1,)),
        ],
        compiler_params=params(),
        cost_estimate=pl.CostEstimate(flops=2 * 16 * blocks * size * size, bytes_accessed=2 * blocks * size * size, transcendentals=0),
        name="interior",
    )(weighted, *pinned(dirichlet_inv, coarse_inv))

    near_rows = NF + LANES + REST + coarse_inv.size // LANES
    local, send, chosen, near, far = pl.pallas_call(
        level2_kernel,
        out_shape=(
            jax.ShapeDtypeStruct((loads, LANES), F32),
            jax.ShapeDtypeStruct((wide, 8, LANES), BF16),
            jax.ShapeDtypeStruct((LANES, LANES), BF16),
            jax.ShapeDtypeStruct((near_rows, LANES), BF16),
            jax.ShapeDtypeStruct((NF + LANES + REST, LANES), BF16),
        ),
        in_specs=[VMEM] * 9,
        out_specs=(VMEM,) * 5,
        scratch_shapes=[
            pltpu.VMEM((8, LANES), F32),
            pltpu.VMEM((REST, LANES), F32),
        ],
        compiler_params=params(),
        name="level2",
    )(parts, level2_inv, level2_basis, fine_index, coarse_index, interior, inverse, basis, tiles)
    far = lax.ppermute(far, "wide", [(i, (((i + 1) ^ 1) - 1) % wide) for i in range(wide)])
    near = lax.ppermute(near, "wide", [(i, i ^ 1) for i in range(wide)])
    packets = lax.all_to_all(send, "wide", 0, 0)
    packets, near, far = lax.optimization_barrier((packets, near, far))

    send, hot, owner = pl.pallas_call(
        functools.partial(coarse_kernel, width=width),
        out_shape=(
            jax.ShapeDtypeStruct((wide // 2, 8, LANES), BF16),
            jax.ShapeDtypeStruct((LANES, 3 * LANES), BF16),
            jax.ShapeDtypeStruct((8, 3 * LANES), F32),
        ),
        in_specs=[VMEM] * 4,
        out_specs=(VMEM,) * 3,
        compiler_params=params(),
        name="coarse",
    )(packets, tiles, coarse_index, near)
    cores = [[chip * 2 + core for chip in range(wide // 2)] for core in range(2)]
    corr = lax.all_to_all(send, "wide", 0, 0, axis_index_groups=cores)

    return pl.pallas_call(
        tail_kernel,
        out_shape=jax.ShapeDtypeStruct((loads, width), F32),
        in_specs=[VMEM] * 10,
        out_specs=hbm,
        scratch_shapes=[pltpu.VMEM((loads, width), F32), pltpu.SemaphoreType.DMA((4,))],
        compiler_params=params(),
        name="tail",
    )(corr, hot, owner, local, chosen, near, far, interior, inverse, basis)


def solution(mesh):
    placed = (
        P(None, ("wide", "narrow")),
        P(("wide", "narrow")),
        P(("wide", "narrow"), None, None),
        P(("wide", "narrow"), None),
        P(("wide", "narrow"), None),
        P("wide", None),
        P("wide", None),
        P("wide", None),
        P("wide", None),
    )
    return jax.shard_map(
        per_device,
        mesh=mesh,
        in_specs=placed,
        out_specs=P(None, ("wide", "narrow")),
        check_vma=False,
    )
```

```python
import functools

import jax
import jax.numpy as jnp
from jax import lax
from jax.experimental import pallas as pl
from jax.experimental.pallas import tpu as pltpu
from jax.sharding import PartitionSpec as P

NF = 1152
LANES = 128
REST = 64
LOCAL = 48
F32 = jnp.float32
BF16 = jnp.bfloat16
LIMIT = 16 * 1024 * 1024
NN = (((1,), (0,)), ((), ()))
NT = (((1,), (1,)), ((), ()))
VMEM = pl.BlockSpec(memory_space=pltpu.VMEM)


def mm(a, b, dims=NN):
    return lax.dot_general(a, b, dims, preferred_element_type=F32)


def split_mm(a, b, dims=NN):
    high = a.astype(BF16).astype(F32)
    mid = (a - high).astype(BF16).astype(F32)
    parts = mm(jnp.concatenate([high, mid, a - high - mid], axis=0).astype(BF16), b, dims)
    rows = a.shape[0]
    return parts[:rows] + (parts[rows : 2 * rows] + parts[2 * rows :])


def side_by_side(a, b):
    zero = jnp.zeros_like(a)
    return jnp.concatenate([jnp.concatenate([a, zero], axis=1), jnp.concatenate([zero, b], axis=1)], axis=0).astype(BF16)


def selector(index_row, width):
    column = jnp.transpose(jnp.broadcast_to(index_row.astype(F32), (LANES, LANES)))
    lane = lax.broadcasted_iota(jnp.int32, (LANES, LANES), 1).astype(F32)
    return jnp.concatenate(
        [jnp.where(column == lane + float(q * LANES), 1.0, 0.0) for q in range(width // LANES)], axis=1
    ).astype(BF16)


def sides(width):
    me, count = lax.axis_index("wide"), lax.axis_size("wide")
    odd = lax.rem(me, 2)
    last = width - NF
    far = me - 1 + 2 * odd
    inside = jnp.logical_and(far >= 0, far < count)
    return (
        (pl.multiple_of(last * (1 - odd), LANES), me + 1 - 2 * odd, None),
        (pl.multiple_of(last * odd, LANES), jnp.clip(far, 0, count - 1), inside),
    )


def copies_of(pairs, sems):
    copies = [pltpu.make_async_copy(source, target, sems.at[at]) for at, (source, target) in enumerate(pairs)]
    for copy in copies:
        copy.start()
    return copies


def head_kernel(
    resid_hbm,
    mult_hbm,
    basis_hbm,
    index_hbm,
    basis_ref,
    weighted_ref,
    inverse_ref,
    send_ref,
    resid_ref,
    mult_ref,
    index_ref,
    sems,
):
    width = resid_ref.shape[1]
    level_width = 4 * LANES
    loads = resid_ref.shape[0]
    parts = sems.shape[0] - 3
    step = width // parts
    cuts = [slice(part * step, (part + 1) * step) for part in range(parts)]
    copies = copies_of(
        [(mult_hbm, mult_ref), (resid_hbm, resid_ref), (index_hbm, index_ref)]
        + [(basis_hbm.at[cut], basis_ref.at[cut]) for cut in cuts],
        sems,
    )
    copies[0].wait()
    inverse = 1.0 / mult_ref[...].astype(F32)
    inverse_ref[...] = inverse
    copies[1].wait()
    weighted = resid_ref[...] * inverse
    weighted_ref[...] = weighted.astype(BF16)
    copies[2].wait()
    select = selector(index_ref[...], level_width)
    total = jnp.zeros((2 * loads, 2 * LANES), F32)
    for part, cut in enumerate(cuts):
        copies[3 + part].wait()
        first, second = slice(cut.start, cut.start + step // 2), slice(cut.start + step // 2, cut.stop)
        total += mm(
            jnp.concatenate([weighted[:, first], weighted[:, second]], axis=0).astype(BF16),
            jnp.concatenate([basis_ref[first, :], basis_ref[second, :]], axis=1),
        )
    total = total[:loads, :LANES] + total[loads:, LANES:]
    contrib = split_mm(total, select)
    chunk = jnp.concatenate(
        [contrib[:, q * LANES : (q + 1) * LANES] for q in range(level_width // LANES)], axis=0
    ).astype(BF16)
    for other in range(send_ref.shape[0]):
        send_ref[other] = chunk


def interior_kernel(weighted_ref, blocks_hbm, coarse_inv_hbm, interior_ref, tiles_ref, blocks_ref, rows_ref, sems, *, spans):
    size = blocks_ref.shape[1]
    whole = size // 256 * 256
    cuts = [pl.ds(first, blocks) for first, blocks in spans]
    copies = copies_of([(coarse_inv_hbm, rows_ref)] + [(blocks_hbm.at[cut], blocks_ref.at[cut]) for cut in cuts], sems)
    copies[0].wait()
    for p in range(tiles_ref.shape[0]):
        rows = [rows_ref[:, (2 * p + i) * LANES : (2 * p + i + 1) * LANES].astype(F32) for i in range(2)]
        tiles_ref[p] = jnp.transpose(jnp.concatenate(rows, axis=0)).astype(BF16)
    for copy, (first, blocks) in zip(copies[1:], spans):
        copy.wait()
        for b in range(first, first + blocks, 2):
            one, two = slice(b * size, (b + 1) * size), slice((b + 1) * size, (b + 2) * size)
            left, right = weighted_ref[:, one].astype(F32), weighted_ref[:, two].astype(F32)
            rest = mm(
                side_by_side(left[:, whole:], right[:, whole:]),
                jnp.concatenate([blocks_ref[b][:, whole:], blocks_ref[b + 1][:, whole:]], axis=1),
                NT,
            )
            loads = left.shape[0]
            first_sum = mm(left[:, :whole].astype(BF16), blocks_ref[b][:, :whole], NT) + rest[:loads]
            second_sum = mm(right[:, :whole].astype(BF16), blocks_ref[b + 1][:, :whole], NT) + rest[loads:]
            interior_ref[:, one] = first_sum.astype(BF16)
            interior_ref[:, two] = second_sum.astype(BF16)


def level2_kernel(
    parts_ref,
    inverse_ref,
    level2_basis_ref,
    index_ref,
    coarse_index_ref,
    interior_ref,
    inverse_mult_ref,
    basis_ref,
    tiles_ref,
    local_ref,
    send_ref,
    picked_ref,
    near_ref,
    far_ref,
    packet,
    stage,
):
    loads, width = interior_ref.shape
    rows = stage.shape[0]
    total = jnp.sum(parts_ref[...].astype(F32), axis=0)
    low = jnp.concatenate([total[q * loads : (q + 1) * loads] for q in range(total.shape[0] // loads)], axis=1).astype(BF16)
    local = mm(low, inverse_ref[...], NT)
    select = selector(index_ref[...], level2_basis_ref.shape[0])
    chosen = jnp.transpose(mm(select, level2_basis_ref[...])).astype(BF16)
    picked_ref[...] = chosen
    local_picked = split_mm(local, select, NT)
    local_ref[...] = local_picked
    coarse = coarse_index_ref[...]
    packet[:loads, :] = mm(low, level2_basis_ref[...])
    packet[loads : loads + 1, :] = (coarse // LANES).astype(F32)
    packet[loads + 1 : loads + 2, :] = (coarse % LANES).astype(F32)
    packet[loads + 2 :, :] = jnp.zeros((packet.shape[0] - loads - 2, LANES), F32)
    chunk = packet[...].astype(BF16)
    for other in range(send_ref.shape[0]):
        send_ref[other] = chunk

    pieces = NF // LANES
    for out_ref, (start, _, _) in zip((near_ref, far_ref), sides(width)):
        out_ref[:NF, :] = basis_ref[pl.ds(start, NF), :]
        out_ref[NF : NF + LANES, :] = chosen
        stage[loads * pieces :, :] = jnp.zeros((rows - loads * pieces, LANES), F32)
        for q in range(pieces):
            lanes = pl.ds(pl.multiple_of(start + q * LANES, LANES), LANES)
            stage[q * loads : (q + 1) * loads, :] = interior_ref[:, lanes].astype(F32)
            stage[loads * pieces + q : loads * pieces + q + 1, :] = jnp.round(1.0 / inverse_mult_ref[:, lanes])
        stage[LOCAL : LOCAL + loads, :] = local_picked
        out_ref[NF + LANES : NF + LANES + rows, :] = stage[...].astype(BF16)
    count = tiles_ref.shape[1]
    for h in range(tiles_ref.shape[0]):
        at = NF + LANES + rows + h * count
        near_ref[at : at + count, :] = tiles_ref[h]


def coarse_kernel(packets_ref, tiles_ref, coarse_index_ref, near_ref, send_ref, hot_ref, owner_ref, *, width):
    loads = 4
    groups, rows = packets_ref.shape[0], packets_ref.shape[1]
    pairs = tiles_ref.shape[0]
    highs, count = 2 * pairs, tiles_ref.shape[2] // 2
    row = lax.broadcasted_iota(jnp.int32, (LANES, LANES), 0).astype(F32).astype(BF16)
    tall, hot = [], []
    for g in range(groups):
        packet = packets_ref[g].astype(F32)
        twice = jnp.concatenate([packet, packet], axis=0).astype(BF16)
        high = jnp.broadcast_to(packet[loads : loads + 1], (2 * rows, LANES))
        which = jnp.concatenate([jnp.zeros((rows, LANES), F32), jnp.ones((rows, LANES), F32)], axis=0)
        high = (high - which).astype(BF16)
        low = jnp.broadcast_to(packet[loads + 1 : loads + 2], (LANES, LANES)).astype(BF16)
        zero, one = jnp.zeros((), BF16), jnp.ones((), BF16)
        tall.append(jnp.concatenate([jnp.where(high == jnp.asarray(h, BF16), twice, zero) for h in range(0, highs, 2)], axis=0))
        hot.append(jnp.where(row == low, one, zero))
    total = mm(jnp.concatenate(tall, axis=1), jnp.concatenate(hot, axis=1), NT)
    coarse_low = jnp.concatenate(
        [jnp.concatenate([total[rows * h : rows * (h + 1)] for h in range(i, highs, 2)], axis=1) for i in range(2)], axis=0
    ).astype(BF16)
    tiles = jnp.concatenate([tiles_ref[p] for p in range(pairs)], axis=0)
    theirs = near_ref[near_ref.shape[0] - pairs * LANES :, :]
    both = mm(coarse_low, jnp.concatenate([tiles, theirs], axis=1))
    own = both[:rows, :count] + both[rows:, count : 2 * count]
    other = both[:rows, 2 * count : 3 * count] + both[rows:, 3 * count :]
    odd = lax.rem(lax.axis_index("wide"), 2) == 1
    chunk = jnp.concatenate([jnp.where(odd, other, own), jnp.where(odd, own, other)], axis=1).astype(BF16)
    for at in range(send_ref.shape[0]):
        send_ref[at] = chunk

    packets = [packets_ref[group].astype(F32) for _, group, _ in sides(width)]
    coarse = coarse_index_ref[...]
    owner = jnp.concatenate([(coarse // LANES).astype(F32)] + [p[loads : loads + 1] for p in packets], axis=1)
    within = jnp.concatenate([(coarse % LANES).astype(F32)] + [p[loads + 1 : loads + 2] for p in packets], axis=1)
    shape = (LANES, within.shape[1])
    lane = lax.broadcasted_iota(jnp.int32, shape, 0).astype(F32)
    hot_ref[...] = jnp.where(lane == jnp.broadcast_to(within, shape), 1.0, 0.0).astype(BF16)
    owner_ref[...] = jnp.broadcast_to(owner, owner_ref.shape)


def tail_kernel(
    corr_ref,
    hot_ref,
    owner_ref,
    local_ref,
    picked_ref,
    near_ref,
    far_ref,
    interior_ref,
    inverse_ref,
    basis_ref,
    out_hbm,
    out_ref,
    sems,
):
    loads, width = interior_ref.shape
    half = width // 2
    pieces = NF // LANES
    chips, rows = corr_ref.shape[0], corr_ref.shape[1]
    table = jnp.concatenate([corr_ref[c].astype(F32) for c in range(chips)], axis=0).astype(BF16)
    picks = mm(table, hot_ref[...])
    owner = owner_ref[...]
    picked = jnp.zeros(owner.shape, F32)
    for c in range(chips):
        picked += jnp.where(owner == float(c), picks[rows * c : rows * (c + 1)], 0.0)
    picked = picked.astype(BF16)
    gathered = local_ref[...] + mm(picked[:, :LANES], picked_ref[...])[:loads]
    gathered = side_by_side(gathered, gathered)
    theirs, rests = [], []
    for side, face_ref in enumerate((near_ref, far_ref)):
        lanes = slice((side + 1) * LANES, (side + 2) * LANES)
        rest = face_ref[NF + LANES : NF + LANES + REST, :].astype(F32)
        theirs.append(rest[LOCAL : LOCAL + loads] + mm(picked[:, lanes], face_ref[NF : NF + LANES, :])[:loads])
        rests.append(rest)
    shifts = mm(side_by_side(*theirs), jnp.concatenate([near_ref[:NF, :], far_ref[:NF, :]], axis=1), NT)

    copies = []

    def piece(one, two):
        shift = mm(gathered, jnp.concatenate([basis_ref[one, :], basis_ref[two, :]], axis=1), NT)
        out_ref[:, one] = (interior_ref[:, one].astype(F32) + shift[:loads]) * inverse_ref[:, one]
        out_ref[:, two] = (interior_ref[:, two].astype(F32) + shift[loads:]) * inverse_ref[:, two]

    def send(cut):
        copy = pltpu.make_async_copy(out_ref.at[:, cut], out_hbm.at[:, cut], sems.at[len(copies)])
        copy.start()
        copies.append(copy)

    faces = []
    for side, (_, _, exists) in enumerate(sides(width)):
        rest, shift = rests[side], shifts[side * loads : (side + 1) * loads]
        weights = jnp.concatenate([rest[loads * pieces + q : loads * pieces + q + 1] for q in range(pieces)], axis=1)
        scale = 1.0 / weights
        if exists is not None:
            scale = jnp.where(exists, scale, 0.0)
        inside = jnp.concatenate([rest[q * loads : (q + 1) * loads] for q in range(pieces)], axis=1)
        faces.append((inside + shift) * scale)
    odd = lax.rem(lax.axis_index("wide"), 2) == 1
    from_below, from_above = jnp.where(odd, faces[0], faces[1]), jnp.where(odd, faces[1], faces[0])

    quarter = width // 4
    ends = slice(0, quarter), slice(width - quarter, width)
    piece(*ends)
    out_ref[:, :NF] = out_ref[:, :NF] + from_below
    out_ref[:, width - NF :] = out_ref[:, width - NF :] + from_above
    send(ends[0])
    send(ends[1])
    middle = slice(quarter, half), slice(half, width - quarter)
    piece(*middle)
    send(middle[0])
    send(middle[1])
    for copy in copies:
        copy.wait()


def params(limit=LIMIT):
    return pltpu.CompilerParams(vmem_limit_bytes=limit)


def per_device(
    resid,
    mult,
    dirichlet_inv,
    fine_basis,
    fine_index,
    level2_inv,
    level2_basis,
    coarse_index,
    coarse_inv,
):
    loads, width = resid.shape
    blocks, size = dirichlet_inv.shape[0], dirichlet_inv.shape[1]
    wide, narrow = lax.axis_size("wide"), lax.axis_size("narrow")
    mult = mult.reshape(1, width)

    pieces = 3
    hbm = pl.BlockSpec(memory_space=pltpu.HBM)

    def pinned(*arrays):
        return [pltpu.with_memory_space_constraint(array, pltpu.HBM) for array in arrays]

    basis, weighted, inverse, send = pl.pallas_call(
        head_kernel,
        out_shape=(
            jax.ShapeDtypeStruct(fine_basis.shape, BF16),
            jax.ShapeDtypeStruct((loads, width), BF16),
            jax.ShapeDtypeStruct((1, width), F32),
            jax.ShapeDtypeStruct((narrow, 16, LANES), BF16),
        ),
        in_specs=[hbm] * 4,
        out_specs=(VMEM,) * 4,
        scratch_shapes=[
            pltpu.VMEM(resid.shape, F32),
            pltpu.VMEM(mult.shape, jnp.int32),
            pltpu.VMEM(fine_index.shape, jnp.int32),
            pltpu.SemaphoreType.DMA((3 + pieces,)),
        ],
        compiler_params=params(),
        name="head",
    )(*pinned(resid, mult, fine_basis, fine_index))
    parts = lax.all_to_all(send, "narrow", 0, 0)
    sixth = blocks // 6
    spans = tuple((at, sixth) for at in range(0, blocks, sixth))
    highs = coarse_inv.shape[1] // LANES
    interior, tiles = pl.pallas_call(
        functools.partial(interior_kernel, spans=spans),
        out_shape=(
            jax.ShapeDtypeStruct((loads, width), BF16),
            jax.ShapeDtypeStruct((highs // 2, LANES, LANES), BF16),
        ),
        input_output_aliases={0: 0},
        in_specs=[VMEM, hbm, hbm],
        out_specs=(VMEM, VMEM),
        scratch_shapes=[
            pltpu.VMEM(dirichlet_inv.shape, BF16),
            pltpu.VMEM(coarse_inv.shape, BF16),
            pltpu.SemaphoreType.DMA((len(spans) + 1,)),
        ],
        compiler_params=params(),
        cost_estimate=pl.CostEstimate(flops=2 * 16 * blocks * size * size, bytes_accessed=2 * blocks * size * size, transcendentals=0),
        name="interior",
    )(weighted, *pinned(dirichlet_inv, coarse_inv))

    near_rows = NF + LANES + REST + coarse_inv.size // LANES
    local, send, chosen, near, far = pl.pallas_call(
        level2_kernel,
        out_shape=(
            jax.ShapeDtypeStruct((loads, LANES), F32),
            jax.ShapeDtypeStruct((wide, 8, LANES), BF16),
            jax.ShapeDtypeStruct((LANES, LANES), BF16),
            jax.ShapeDtypeStruct((near_rows, LANES), BF16),
            jax.ShapeDtypeStruct((NF + LANES + REST, LANES), BF16),
        ),
        in_specs=[VMEM] * 9,
        out_specs=(VMEM,) * 5,
        scratch_shapes=[
            pltpu.VMEM((8, LANES), F32),
            pltpu.VMEM((REST, LANES), F32),
        ],
        compiler_params=params(),
        name="level2",
    )(parts, level2_inv, level2_basis, fine_index, coarse_index, interior, inverse, basis, tiles)
    far = lax.ppermute(far, "wide", [(i, (((i + 1) ^ 1) - 1) % wide) for i in range(wide)])
    near = lax.ppermute(near, "wide", [(i, i ^ 1) for i in range(wide)])
    packets = lax.all_to_all(send, "wide", 0, 0)
    packets, near, far = lax.optimization_barrier((packets, near, far))

    send, hot, owner = pl.pallas_call(
        functools.partial(coarse_kernel, width=width),
        out_shape=(
            jax.ShapeDtypeStruct((wide // 2, 8, LANES), BF16),
            jax.ShapeDtypeStruct((LANES, 3 * LANES), BF16),
            jax.ShapeDtypeStruct((8, 3 * LANES), F32),
        ),
        in_specs=[VMEM] * 4,
        out_specs=(VMEM,) * 3,
        compiler_params=params(),
        name="coarse",
    )(packets, tiles, coarse_index, near)
    cores = [[chip * 2 + core for chip in range(wide // 2)] for core in range(2)]
    corr = lax.all_to_all(send, "wide", 0, 0, axis_index_groups=cores)

    return pl.pallas_call(
        tail_kernel,
        out_shape=jax.ShapeDtypeStruct((loads, width), F32),
        in_specs=[VMEM] * 10,
        out_specs=hbm,
        scratch_shapes=[pltpu.VMEM((loads, width), F32), pltpu.SemaphoreType.DMA((4,))],
        compiler_params=params(),
        name="tail",
    )(corr, hot, owner, local, chosen, near, far, interior, inverse, basis)


def solution(mesh):
    placed = (
        P(None, ("wide", "narrow")),
        P(("wide", "narrow")),
        P(("wide", "narrow"), None, None),
        P(("wide", "narrow"), None),
        P(("wide", "narrow"), None),
        P("wide", None),
        P("wide", None),
        P("wide", None),
        P("wide", None),
    )
    return jax.shard_map(
        per_device,
        mesh=mesh,
        in_specs=placed,
        out_specs=P(None, ("wide", "narrow")),
        check_vma=False,
    )
```

```python
import functools

import jax
import jax.numpy as jnp
from jax import lax
from jax.experimental import pallas as pl
from jax.experimental.pallas import tpu as pltpu
from jax.sharding import PartitionSpec as P

NF = 1152
LANES = 128
REST = 64
LOCAL = 48
F32 = jnp.float32
BF16 = jnp.bfloat16
LIMIT = 16 * 1024 * 1024
NN = (((1,), (0,)), ((), ()))
NT = (((1,), (1,)), ((), ()))
VMEM = pl.BlockSpec(memory_space=pltpu.VMEM)


def mm(a, b, dims=NN):
    return lax.dot_general(a, b, dims, preferred_element_type=F32)


def split_mm(a, b, dims=NN):
    high = a.astype(BF16).astype(F32)
    mid = (a - high).astype(BF16).astype(F32)
    parts = mm(jnp.concatenate([high, mid, a - high - mid], axis=0).astype(BF16), b, dims)
    rows = a.shape[0]
    return parts[:rows] + (parts[rows : 2 * rows] + parts[2 * rows :])


def side_by_side(a, b):
    zero = jnp.zeros_like(a)
    return jnp.concatenate([jnp.concatenate([a, zero], axis=1), jnp.concatenate([zero, b], axis=1)], axis=0).astype(BF16)


def selector(index_row, width):
    column = jnp.transpose(jnp.broadcast_to(index_row.astype(F32), (LANES, LANES)))
    lane = lax.broadcasted_iota(jnp.int32, (LANES, LANES), 1).astype(F32)
    return jnp.concatenate(
        [jnp.where(column == lane + float(q * LANES), 1.0, 0.0) for q in range(width // LANES)], axis=1
    ).astype(BF16)


def sides(width):
    me, count = lax.axis_index("wide"), lax.axis_size("wide")
    odd = lax.rem(me, 2)
    last = width - NF
    far = me - 1 + 2 * odd
    inside = jnp.logical_and(far >= 0, far < count)
    return (
        (pl.multiple_of(last * (1 - odd), LANES), me + 1 - 2 * odd, None),
        (pl.multiple_of(last * odd, LANES), jnp.clip(far, 0, count - 1), inside),
    )


def copies_of(pairs, sems):
    copies = [pltpu.make_async_copy(source, target, sems.at[at]) for at, (source, target) in enumerate(pairs)]
    for copy in copies:
        copy.start()
    return copies


def head_kernel(
    resid_hbm,
    mult_hbm,
    basis_hbm,
    index_hbm,
    basis_ref,
    weighted_ref,
    inverse_ref,
    send_ref,
    resid_ref,
    mult_ref,
    index_ref,
    sems,
):
    width = resid_ref.shape[1]
    level_width = 4 * LANES
    loads = resid_ref.shape[0]
    parts = sems.shape[0] - 3
    step = width // parts
    cuts = [slice(part * step, (part + 1) * step) for part in range(parts)]
    copies = copies_of(
        [(mult_hbm, mult_ref), (resid_hbm, resid_ref), (index_hbm, index_ref)]
        + [(basis_hbm.at[cut], basis_ref.at[cut]) for cut in cuts],
        sems,
    )
    copies[0].wait()
    inverse = 1.0 / mult_ref[...].astype(F32)
    inverse_ref[...] = inverse
    copies[1].wait()
    weighted = resid_ref[...] * inverse
    weighted_ref[...] = weighted.astype(BF16)
    copies[2].wait()
    select = selector(index_ref[...], level_width)
    total = jnp.zeros((2 * loads, 2 * LANES), F32)
    for part, cut in enumerate(cuts):
        copies[3 + part].wait()
        first, second = slice(cut.start, cut.start + step // 2), slice(cut.start + step // 2, cut.stop)
        total += mm(
            jnp.concatenate([weighted[:, first], weighted[:, second]], axis=0).astype(BF16),
            jnp.concatenate([basis_ref[first, :], basis_ref[second, :]], axis=1),
        )
    total = total[:loads, :LANES] + total[loads:, LANES:]
    contrib = split_mm(total, select)
    chunk = jnp.concatenate(
        [contrib[:, q * LANES : (q + 1) * LANES] for q in range(level_width // LANES)], axis=0
    ).astype(BF16)
    for other in range(send_ref.shape[0]):
        send_ref[other] = chunk


def interior_kernel(weighted_ref, blocks_hbm, coarse_inv_hbm, interior_ref, tiles_ref, blocks_ref, rows_ref, sems, *, spans):
    size = blocks_ref.shape[1]
    whole = size // 256 * 256
    cuts = [pl.ds(first, blocks) for first, blocks in spans]
    copies = copies_of([(coarse_inv_hbm, rows_ref)] + [(blocks_hbm.at[cut], blocks_ref.at[cut]) for cut in cuts], sems)
    copies[0].wait()
    for p in range(tiles_ref.shape[0]):
        rows = [rows_ref[:, (2 * p + i) * LANES : (2 * p + i + 1) * LANES].astype(F32) for i in range(2)]
        tiles_ref[p] = jnp.transpose(jnp.concatenate(rows, axis=0)).astype(BF16)
    for copy, (first, blocks) in zip(copies[1:], spans):
        copy.wait()
        for b in range(first, first + blocks, 2):
            one, two = slice(b * size, (b + 1) * size), slice((b + 1) * size, (b + 2) * size)
            left, right = weighted_ref[:, one].astype(F32), weighted_ref[:, two].astype(F32)
            rest = mm(
                side_by_side(left[:, whole:], right[:, whole:]),
                jnp.concatenate([blocks_ref[b][:, whole:], blocks_ref[b + 1][:, whole:]], axis=1),
                NT,
            )
            loads = left.shape[0]
            first_sum = mm(left[:, :whole].astype(BF16), blocks_ref[b][:, :whole], NT) + rest[:loads]
            second_sum = mm(right[:, :whole].astype(BF16), blocks_ref[b + 1][:, :whole], NT) + rest[loads:]
            interior_ref[:, one] = first_sum.astype(BF16)
            interior_ref[:, two] = second_sum.astype(BF16)


def level2_kernel(
    parts_ref,
    inverse_ref,
    level2_basis_ref,
    index_ref,
    coarse_index_ref,
    interior_ref,
    inverse_mult_ref,
    basis_ref,
    tiles_ref,
    local_ref,
    send_ref,
    picked_ref,
    near_ref,
    far_ref,
    packet,
    stage,
):
    loads, width = interior_ref.shape
    rows = stage.shape[0]
    total = jnp.sum(parts_ref[...].astype(F32), axis=0)
    low = jnp.concatenate([total[q * loads : (q + 1) * loads] for q in range(total.shape[0] // loads)], axis=1).astype(BF16)
    local = mm(low, inverse_ref[...], NT)
    select = selector(index_ref[...], level2_basis_ref.shape[0])
    chosen = jnp.transpose(mm(select, level2_basis_ref[...])).astype(BF16)
    picked_ref[...] = chosen
    local_picked = split_mm(local, select, NT)
    local_ref[...] = local_picked
    coarse = coarse_index_ref[...]
    packet[:loads, :] = mm(low, level2_basis_ref[...])
    packet[loads : loads + 1, :] = (coarse // LANES).astype(F32)
    packet[loads + 1 : loads + 2, :] = (coarse % LANES).astype(F32)
    packet[loads + 2 :, :] = jnp.zeros((packet.shape[0] - loads - 2, LANES), F32)
    chunk = packet[...].astype(BF16)
    for other in range(send_ref.shape[0]):
        send_ref[other] = chunk

    pieces = NF // LANES
    for out_ref, (start, _, _) in zip((near_ref, far_ref), sides(width)):
        out_ref[:NF, :] = basis_ref[pl.ds(start, NF), :]
        out_ref[NF : NF + LANES, :] = chosen
        stage[loads * pieces :, :] = jnp.zeros((rows - loads * pieces, LANES), F32)
        for q in range(pieces):
            lanes = pl.ds(pl.multiple_of(start + q * LANES, LANES), LANES)
            stage[q * loads : (q + 1) * loads, :] = interior_ref[:, lanes].astype(F32)
            stage[loads * pieces + q : loads * pieces + q + 1, :] = jnp.round(1.0 / inverse_mult_ref[:, lanes])
        stage[LOCAL : LOCAL + loads, :] = local_picked
        out_ref[NF + LANES : NF + LANES + rows, :] = stage[...].astype(BF16)
    count = tiles_ref.shape[1]
    for h in range(tiles_ref.shape[0]):
        at = NF + LANES + rows + h * count
        near_ref[at : at + count, :] = tiles_ref[h]


def coarse_kernel(packets_ref, tiles_ref, coarse_index_ref, near_ref, send_ref, hot_ref, owner_ref, *, width):
    loads = 4
    groups, rows = packets_ref.shape[0], packets_ref.shape[1]
    pairs = tiles_ref.shape[0]
    highs, count = 2 * pairs, tiles_ref.shape[2] // 2
    row = lax.broadcasted_iota(jnp.int32, (LANES, LANES), 0).astype(F32).astype(BF16)
    tall, hot = [], []
    for g in range(groups):
        packet = packets_ref[g].astype(F32)
        twice = jnp.concatenate([packet, packet], axis=0).astype(BF16)
        high = jnp.broadcast_to(packet[loads : loads + 1], (2 * rows, LANES))
        which = jnp.concatenate([jnp.zeros((rows, LANES), F32), jnp.ones((rows, LANES), F32)], axis=0)
        high = (high - which).astype(BF16)
        low = jnp.broadcast_to(packet[loads + 1 : loads + 2], (LANES, LANES)).astype(BF16)
        zero, one = jnp.zeros((), BF16), jnp.ones((), BF16)
        tall.append(jnp.concatenate([jnp.where(high == jnp.asarray(h, BF16), twice, zero) for h in range(0, highs, 2)], axis=0))
        hot.append(jnp.where(row == low, one, zero))
    total = mm(jnp.concatenate(tall, axis=1), jnp.concatenate(hot, axis=1), NT)
    coarse_low = jnp.concatenate(
        [jnp.concatenate([total[rows * h : rows * (h + 1)] for h in range(i, highs, 2)], axis=1) for i in range(2)], axis=0
    ).astype(BF16)
    tiles = jnp.concatenate([tiles_ref[p] for p in range(pairs)], axis=0)
    theirs = near_ref[near_ref.shape[0] - pairs * LANES :, :]
    both = mm(coarse_low, jnp.concatenate([tiles, theirs], axis=1))
    own = both[:rows, :count] + both[rows:, count : 2 * count]
    other = both[:rows, 2 * count : 3 * count] + both[rows:, 3 * count :]
    odd = lax.rem(lax.axis_index("wide"), 2) == 1
    chunk = jnp.concatenate([jnp.where(odd, other, own), jnp.where(odd, own, other)], axis=1)[:loads].astype(BF16)
    for at in range(send_ref.shape[0]):
        send_ref[at] = chunk

    packets = [packets_ref[group].astype(F32) for _, group, _ in sides(width)]
    coarse = coarse_index_ref[...]
    owner = jnp.concatenate([(coarse // LANES).astype(F32)] + [p[loads : loads + 1] for p in packets], axis=1)
    within = jnp.concatenate([(coarse % LANES).astype(F32)] + [p[loads + 1 : loads + 2] for p in packets], axis=1)
    shape = (LANES, within.shape[1])
    lane = lax.broadcasted_iota(jnp.int32, shape, 0).astype(F32)
    hot_ref[...] = jnp.where(lane == jnp.broadcast_to(within, shape), 1.0, 0.0).astype(BF16)
    owner_ref[...] = jnp.broadcast_to(owner, owner_ref.shape)


def tail_kernel(
    corr_ref,
    hot_ref,
    owner_ref,
    local_ref,
    picked_ref,
    near_ref,
    far_ref,
    interior_ref,
    inverse_ref,
    basis_ref,
    out_hbm,
    out_ref,
    sems,
):
    loads, width = interior_ref.shape
    half = width // 2
    pieces = NF // LANES
    chips = corr_ref.shape[0]
    table = jnp.concatenate([corr_ref[c].astype(F32) for c in range(chips)], axis=0).astype(BF16)
    picks = mm(table, hot_ref[...])
    owner = owner_ref[...]
    owner = owner - jnp.where(lax.broadcasted_iota(jnp.int32, owner.shape, 0) >= loads, 1.0, 0.0)
    picked = jnp.zeros(owner.shape, F32)
    for c in range(0, chips, 2):
        picked += jnp.where(owner == float(c), picks[loads * c : loads * (c + 2)], 0.0)
    picked = (picked[:loads] + picked[loads:]).astype(BF16)
    gathered = local_ref[...] + mm(picked[:, :LANES], picked_ref[...])[:loads]
    gathered = side_by_side(gathered, gathered)
    theirs, rests = [], []
    for side, face_ref in enumerate((near_ref, far_ref)):
        lanes = slice((side + 1) * LANES, (side + 2) * LANES)
        rest = face_ref[NF + LANES : NF + LANES + REST, :].astype(F32)
        theirs.append(rest[LOCAL : LOCAL + loads] + mm(picked[:, lanes], face_ref[NF : NF + LANES, :])[:loads])
        rests.append(rest)
    shifts = mm(side_by_side(*theirs), jnp.concatenate([near_ref[:NF, :], far_ref[:NF, :]], axis=1), NT)

    copies = []

    def piece(one, two):
        shift = mm(gathered, jnp.concatenate([basis_ref[one, :], basis_ref[two, :]], axis=1), NT)
        out_ref[:, one] = (interior_ref[:, one].astype(F32) + shift[:loads]) * inverse_ref[:, one]
        out_ref[:, two] = (interior_ref[:, two].astype(F32) + shift[loads:]) * inverse_ref[:, two]

    def send(cut):
        copy = pltpu.make_async_copy(out_ref.at[:, cut], out_hbm.at[:, cut], sems.at[len(copies)])
        copy.start()
        copies.append(copy)

    faces = []
    for side, (_, _, exists) in enumerate(sides(width)):
        rest, shift = rests[side], shifts[side * loads : (side + 1) * loads]
        weights = jnp.concatenate([rest[loads * pieces + q : loads * pieces + q + 1] for q in range(pieces)], axis=1)
        scale = 1.0 / weights
        if exists is not None:
            scale = jnp.where(exists, scale, 0.0)
        inside = jnp.concatenate([rest[q * loads : (q + 1) * loads] for q in range(pieces)], axis=1)
        faces.append((inside + shift) * scale)
    odd = lax.rem(lax.axis_index("wide"), 2) == 1
    from_below, from_above = jnp.where(odd, faces[0], faces[1]), jnp.where(odd, faces[1], faces[0])

    quarter = width // 4
    ends = slice(0, quarter), slice(width - quarter, width)
    piece(*ends)
    out_ref[:, :NF] = out_ref[:, :NF] + from_below
    out_ref[:, width - NF :] = out_ref[:, width - NF :] + from_above
    send(ends[0])
    send(ends[1])
    piece(slice(quarter, half), slice(half, width - quarter))
    send(slice(quarter, width - quarter))
    for copy in copies:
        copy.wait()


def params(limit=LIMIT):
    return pltpu.CompilerParams(vmem_limit_bytes=limit)


def per_device(
    resid,
    mult,
    dirichlet_inv,
    fine_basis,
    fine_index,
    level2_inv,
    level2_basis,
    coarse_index,
    coarse_inv,
):
    loads, width = resid.shape
    blocks, size = dirichlet_inv.shape[0], dirichlet_inv.shape[1]
    wide, narrow = lax.axis_size("wide"), lax.axis_size("narrow")
    mult = mult.reshape(1, width)

    pieces = 3
    hbm = pl.BlockSpec(memory_space=pltpu.HBM)

    def pinned(*arrays):
        return [pltpu.with_memory_space_constraint(array, pltpu.HBM) for array in arrays]

    basis, weighted, inverse, send = pl.pallas_call(
        head_kernel,
        out_shape=(
            jax.ShapeDtypeStruct(fine_basis.shape, BF16),
            jax.ShapeDtypeStruct((loads, width), BF16),
            jax.ShapeDtypeStruct((1, width), F32),
            jax.ShapeDtypeStruct((narrow, 16, LANES), BF16),
        ),
        in_specs=[hbm] * 4,
        out_specs=(VMEM,) * 4,
        scratch_shapes=[
            pltpu.VMEM(resid.shape, F32),
            pltpu.VMEM(mult.shape, jnp.int32),
            pltpu.VMEM(fine_index.shape, jnp.int32),
            pltpu.SemaphoreType.DMA((3 + pieces,)),
        ],
        compiler_params=params(),
        name="head",
    )(*pinned(resid, mult, fine_basis, fine_index))
    parts = lax.all_to_all(send, "narrow", 0, 0)
    sixth = blocks // 6
    spans = tuple((at, sixth) for at in range(0, blocks, sixth))
    highs = coarse_inv.shape[1] // LANES
    interior, tiles = pl.pallas_call(
        functools.partial(interior_kernel, spans=spans),
        out_shape=(
            jax.ShapeDtypeStruct((loads, width), BF16),
            jax.ShapeDtypeStruct((highs // 2, LANES, LANES), BF16),
        ),
        input_output_aliases={0: 0},
        in_specs=[VMEM, hbm, hbm],
        out_specs=(VMEM, VMEM),
        scratch_shapes=[
            pltpu.VMEM(dirichlet_inv.shape, BF16),
            pltpu.VMEM(coarse_inv.shape, BF16),
            pltpu.SemaphoreType.DMA((len(spans) + 1,)),
        ],
        compiler_params=params(),
        cost_estimate=pl.CostEstimate(flops=2 * 16 * blocks * size * size, bytes_accessed=2 * blocks * size * size, transcendentals=0),
        name="interior",
    )(weighted, *pinned(dirichlet_inv, coarse_inv))

    near_rows = NF + LANES + REST + coarse_inv.size // LANES
    local, send, chosen, near, far = pl.pallas_call(
        level2_kernel,
        out_shape=(
            jax.ShapeDtypeStruct((loads, LANES), F32),
            jax.ShapeDtypeStruct((wide, 8, LANES), BF16),
            jax.ShapeDtypeStruct((LANES, LANES), BF16),
            jax.ShapeDtypeStruct((near_rows, LANES), BF16),
            jax.ShapeDtypeStruct((NF + LANES + REST, LANES), BF16),
        ),
        in_specs=[VMEM] * 9,
        out_specs=(VMEM,) * 5,
        scratch_shapes=[
            pltpu.VMEM((8, LANES), F32),
            pltpu.VMEM((REST, LANES), F32),
        ],
        compiler_params=params(),
        name="level2",
    )(parts, level2_inv, level2_basis, fine_index, coarse_index, interior, inverse, basis, tiles)
    far = lax.ppermute(far, "wide", [(i, (((i + 1) ^ 1) - 1) % wide) for i in range(wide)])
    near = lax.ppermute(near, "wide", [(i, i ^ 1) for i in range(wide)])
    packets = lax.all_to_all(send, "wide", 0, 0)
    packets, near, far = lax.optimization_barrier((packets, near, far))

    send, hot, owner = pl.pallas_call(
        functools.partial(coarse_kernel, width=width),
        out_shape=(
            jax.ShapeDtypeStruct((wide // 2, loads, LANES), BF16),
            jax.ShapeDtypeStruct((LANES, 3 * LANES), BF16),
            jax.ShapeDtypeStruct((8, 3 * LANES), F32),
        ),
        in_specs=[VMEM] * 4,
        out_specs=(VMEM,) * 3,
        compiler_params=params(),
        name="coarse",
    )(packets, tiles, coarse_index, near)
    cores = [[chip * 2 + core for chip in range(wide // 2)] for core in range(2)]
    corr = lax.all_to_all(send, "wide", 0, 0, axis_index_groups=cores)

    return pl.pallas_call(
        tail_kernel,
        out_shape=jax.ShapeDtypeStruct((loads, width), F32),
        in_specs=[VMEM] * 10,
        out_specs=hbm,
        scratch_shapes=[pltpu.VMEM((loads, width), F32), pltpu.SemaphoreType.DMA((3,))],
        compiler_params=params(),
        name="tail",
    )(corr, hot, owner, local, chosen, near, far, interior, inverse, basis)


def solution(mesh):
    placed = (
        P(None, ("wide", "narrow")),
        P(("wide", "narrow")),
        P(("wide", "narrow"), None, None),
        P(("wide", "narrow"), None),
        P(("wide", "narrow"), None),
        P("wide", None),
        P("wide", None),
        P("wide", None),
        P("wide", None),
    )
    return jax.shard_map(
        per_device,
        mesh=mesh,
        in_specs=placed,
        out_specs=P(None, ("wide", "narrow")),
        check_vma=False,
    )
```

```python
import functools

import jax
import jax.numpy as jnp
from jax import lax
from jax.experimental import pallas as pl
from jax.experimental.pallas import tpu as pltpu
from jax.sharding import PartitionSpec as P

NF = 1152
LANES = 128
REST = 64
LOCAL = 48
F32 = jnp.float32
BF16 = jnp.bfloat16
LIMIT = 16 * 1024 * 1024
NN = (((1,), (0,)), ((), ()))
NT = (((1,), (1,)), ((), ()))
VMEM = pl.BlockSpec(memory_space=pltpu.VMEM)


def mm(a, b, dims=NN):
    return lax.dot_general(a, b, dims, preferred_element_type=F32)


def split_mm(a, b, dims=NN):
    high = a.astype(BF16).astype(F32)
    mid = (a - high).astype(BF16).astype(F32)
    parts = mm(jnp.concatenate([high, mid, a - high - mid], axis=0).astype(BF16), b, dims)
    rows = a.shape[0]
    return parts[:rows] + (parts[rows : 2 * rows] + parts[2 * rows :])


def side_by_side(a, b):
    zero = jnp.zeros_like(a)
    return jnp.concatenate([jnp.concatenate([a, zero], axis=1), jnp.concatenate([zero, b], axis=1)], axis=0).astype(BF16)


def selector(index_row, width):
    column = jnp.transpose(jnp.broadcast_to(index_row.astype(F32), (LANES, LANES)))
    lane = lax.broadcasted_iota(jnp.int32, (LANES, LANES), 1).astype(F32)
    return jnp.concatenate(
        [jnp.where(column == lane + float(q * LANES), 1.0, 0.0) for q in range(width // LANES)], axis=1
    ).astype(BF16)


def sides(width):
    me, count = lax.axis_index("wide"), lax.axis_size("wide")
    odd = lax.rem(me, 2)
    last = width - NF
    far = me - 1 + 2 * odd
    inside = jnp.logical_and(far >= 0, far < count)
    return (
        (pl.multiple_of(last * (1 - odd), LANES), me + 1 - 2 * odd, None),
        (pl.multiple_of(last * odd, LANES), jnp.clip(far, 0, count - 1), inside),
    )


def copies_of(pairs, sems):
    copies = [pltpu.make_async_copy(source, target, sems.at[at]) for at, (source, target) in enumerate(pairs)]
    for copy in copies:
        copy.start()
    return copies


def head_kernel(
    resid_hbm,
    mult_hbm,
    basis_hbm,
    index_hbm,
    basis_ref,
    weighted_ref,
    inverse_ref,
    send_ref,
    resid_ref,
    mult_ref,
    index_ref,
    sems,
):
    width = resid_ref.shape[1]
    level_width = 4 * LANES
    loads = resid_ref.shape[0]
    parts = sems.shape[0] - 3
    step = width // parts
    cuts = [slice(part * step, (part + 1) * step) for part in range(parts)]
    copies = copies_of(
        [(mult_hbm, mult_ref), (resid_hbm, resid_ref), (index_hbm, index_ref)]
        + [(basis_hbm.at[cut], basis_ref.at[cut]) for cut in cuts],
        sems,
    )
    copies[0].wait()
    inverse = 1.0 / mult_ref[...].astype(F32)
    inverse_ref[...] = inverse
    copies[1].wait()
    weighted = resid_ref[...] * inverse
    weighted_ref[...] = weighted.astype(BF16)
    copies[2].wait()
    select = selector(index_ref[...], level_width)
    total = jnp.zeros((2 * loads, 2 * LANES), F32)
    for part, cut in enumerate(cuts):
        copies[3 + part].wait()
        first, second = slice(cut.start, cut.start + step // 2), slice(cut.start + step // 2, cut.stop)
        total += mm(
            jnp.concatenate([weighted[:, first], weighted[:, second]], axis=0).astype(BF16),
            jnp.concatenate([basis_ref[first, :], basis_ref[second, :]], axis=1),
        )
    total = total[:loads, :LANES] + total[loads:, LANES:]
    contrib = split_mm(total, select)
    chunk = jnp.concatenate(
        [contrib[:, q * LANES : (q + 1) * LANES] for q in range(level_width // LANES)], axis=0
    ).astype(BF16)
    for other in range(send_ref.shape[0]):
        send_ref[other] = chunk


def interior_kernel(weighted_ref, blocks_hbm, coarse_inv_hbm, interior_ref, tiles_ref, blocks_ref, rows_ref, sems, *, spans):
    size = blocks_ref.shape[1]
    whole = size // 256 * 256
    cuts = [pl.ds(first, blocks) for first, blocks in spans]
    copies = copies_of([(coarse_inv_hbm, rows_ref)] + [(blocks_hbm.at[cut], blocks_ref.at[cut]) for cut in cuts], sems)
    copies[0].wait()
    for p in range(tiles_ref.shape[0]):
        rows = [rows_ref[:, (2 * p + i) * LANES : (2 * p + i + 1) * LANES].astype(F32) for i in range(2)]
        tiles_ref[p] = jnp.transpose(jnp.concatenate(rows, axis=0)).astype(BF16)
    for copy, (first, blocks) in zip(copies[1:], spans):
        copy.wait()
        for b in range(first, first + blocks, 2):
            one, two = slice(b * size, (b + 1) * size), slice((b + 1) * size, (b + 2) * size)
            left, right = weighted_ref[:, one].astype(F32), weighted_ref[:, two].astype(F32)
            rest = mm(
                side_by_side(left[:, whole:], right[:, whole:]),
                jnp.concatenate([blocks_ref[b][:, whole:], blocks_ref[b + 1][:, whole:]], axis=1),
                NT,
            )
            loads = left.shape[0]
            first_sum = mm(left[:, :whole].astype(BF16), blocks_ref[b][:, :whole], NT) + rest[:loads]
            second_sum = mm(right[:, :whole].astype(BF16), blocks_ref[b + 1][:, :whole], NT) + rest[loads:]
            interior_ref[:, one] = first_sum.astype(BF16)
            interior_ref[:, two] = second_sum.astype(BF16)


def level2_kernel(
    parts_ref,
    inverse_ref,
    level2_basis_ref,
    index_ref,
    coarse_index_ref,
    interior_ref,
    inverse_mult_ref,
    basis_ref,
    tiles_ref,
    local_ref,
    send_ref,
    picked_ref,
    near_ref,
    far_ref,
    packet,
    stage,
):
    loads, width = interior_ref.shape
    rows = stage.shape[0]
    total = jnp.sum(parts_ref[...].astype(F32), axis=0)
    low = jnp.concatenate([total[q * loads : (q + 1) * loads] for q in range(total.shape[0] // loads)], axis=1).astype(BF16)
    local = mm(low, inverse_ref[...], NT)
    select = selector(index_ref[...], level2_basis_ref.shape[0])
    chosen = jnp.transpose(mm(select, level2_basis_ref[...])).astype(BF16)
    picked_ref[...] = chosen
    local_picked = split_mm(local, select, NT)
    local_ref[...] = local_picked
    coarse = coarse_index_ref[...]
    packet[:loads, :] = mm(low, level2_basis_ref[...])
    packet[loads : loads + 1, :] = (coarse // LANES).astype(F32)
    packet[loads + 1 : loads + 2, :] = (coarse % LANES).astype(F32)
    packet[loads + 2 :, :] = jnp.zeros((packet.shape[0] - loads - 2, LANES), F32)
    chunk = packet[...].astype(BF16)
    for other in range(send_ref.shape[0]):
        send_ref[other] = chunk

    pieces = NF // LANES
    for out_ref, (start, _, _) in zip((near_ref, far_ref), sides(width)):
        out_ref[:NF, :] = basis_ref[pl.ds(start, NF), :]
        out_ref[NF : NF + LANES, :] = chosen
        stage[loads * pieces :, :] = jnp.zeros((rows - loads * pieces, LANES), F32)
        for q in range(pieces):
            lanes = pl.ds(pl.multiple_of(start + q * LANES, LANES), LANES)
            stage[q * loads : (q + 1) * loads, :] = interior_ref[:, lanes].astype(F32)
            stage[loads * pieces + q : loads * pieces + q + 1, :] = jnp.round(1.0 / inverse_mult_ref[:, lanes])
        stage[LOCAL : LOCAL + loads, :] = local_picked
        out_ref[NF + LANES : NF + LANES + rows, :] = stage[...].astype(BF16)
    count = tiles_ref.shape[1]
    for h in range(tiles_ref.shape[0]):
        at = NF + LANES + rows + h * count
        near_ref[at : at + count, :] = tiles_ref[h]


def coarse_kernel(packets_ref, tiles_ref, coarse_index_ref, near_ref, send_ref, hot_ref, owner_ref, *, width):
    loads = 4
    groups = packets_ref.shape[0]
    pairs = tiles_ref.shape[0]
    highs, count = 2 * pairs, tiles_ref.shape[2] // 2
    row = lax.broadcasted_iota(jnp.int32, (LANES, LANES), 0).astype(F32).astype(BF16)
    which = jnp.concatenate([jnp.full((loads, LANES), float(i), F32) for i in range(4)], axis=0)
    tall, hot = [], []
    for g in range(groups):
        packet = packets_ref[g].astype(F32)
        four = jnp.concatenate([packet[:loads]] * 4, axis=0).astype(BF16)
        high = jnp.broadcast_to(packet[loads : loads + 1], (4 * loads, LANES))
        high = (high - which).astype(BF16)
        low = jnp.broadcast_to(packet[loads + 1 : loads + 2], (LANES, LANES)).astype(BF16)
        zero, one = jnp.zeros((), BF16), jnp.ones((), BF16)
        tall.append(jnp.concatenate([jnp.where(high == jnp.asarray(h, BF16), four, zero) for h in range(0, highs, 4)], axis=0))
        hot.append(jnp.where(row == low, one, zero))
    total = mm(jnp.concatenate(tall, axis=1), jnp.concatenate(hot, axis=1), NT)
    coarse_low = jnp.concatenate(
        [jnp.concatenate([total[loads * h : loads * (h + 1)] for h in range(i, highs, 2)], axis=1) for i in range(2)], axis=0
    ).astype(BF16)
    tiles = jnp.concatenate([tiles_ref[p] for p in range(pairs)], axis=0)
    theirs = near_ref[near_ref.shape[0] - pairs * LANES :, :]
    both = mm(coarse_low, jnp.concatenate([tiles, theirs], axis=1))
    own = both[:loads, :count] + both[loads:, count : 2 * count]
    other = both[:loads, 2 * count : 3 * count] + both[loads:, 3 * count :]
    odd = lax.rem(lax.axis_index("wide"), 2) == 1
    chunk = jnp.concatenate([jnp.where(odd, other, own), jnp.where(odd, own, other)], axis=1).astype(BF16)
    for at in range(send_ref.shape[0]):
        send_ref[at] = chunk

    packets = [packets_ref[group].astype(F32) for _, group, _ in sides(width)]
    coarse = coarse_index_ref[...]
    owner = jnp.concatenate([(coarse // LANES).astype(F32)] + [p[loads : loads + 1] for p in packets], axis=1)
    within = jnp.concatenate([(coarse % LANES).astype(F32)] + [p[loads + 1 : loads + 2] for p in packets], axis=1)
    shape = (LANES, within.shape[1])
    lane = lax.broadcasted_iota(jnp.int32, shape, 0).astype(F32)
    hot_ref[...] = jnp.where(lane == jnp.broadcast_to(within, shape), 1.0, 0.0).astype(BF16)
    owner_ref[...] = jnp.broadcast_to(owner, owner_ref.shape)


def tail_kernel(
    corr_ref,
    hot_ref,
    owner_ref,
    local_ref,
    picked_ref,
    near_ref,
    far_ref,
    interior_ref,
    inverse_ref,
    basis_ref,
    out_hbm,
    out_ref,
    sems,
):
    loads, width = interior_ref.shape
    half = width // 2
    pieces = NF // LANES
    chips = corr_ref.shape[0]
    table = jnp.concatenate([corr_ref[c].astype(F32) for c in range(chips)], axis=0).astype(BF16)
    picks = mm(table, hot_ref[...])
    owner = owner_ref[...]
    owner = owner - jnp.where(lax.broadcasted_iota(jnp.int32, owner.shape, 0) >= loads, 1.0, 0.0)
    picked = jnp.zeros(owner.shape, F32)
    for c in range(0, chips, 2):
        picked += jnp.where(owner == float(c), picks[loads * c : loads * (c + 2)], 0.0)
    picked = (picked[:loads] + picked[loads:]).astype(BF16)
    gathered = local_ref[...] + mm(picked[:, :LANES], picked_ref[...])[:loads]
    gathered = side_by_side(gathered, gathered)
    theirs, rests = [], []
    for side, face_ref in enumerate((near_ref, far_ref)):
        lanes = slice((side + 1) * LANES, (side + 2) * LANES)
        rest = face_ref[NF + LANES : NF + LANES + REST, :].astype(F32)
        theirs.append(rest[LOCAL : LOCAL + loads] + mm(picked[:, lanes], face_ref[NF : NF + LANES, :])[:loads])
        rests.append(rest)
    shifts = mm(side_by_side(*theirs), jnp.concatenate([near_ref[:NF, :], far_ref[:NF, :]], axis=1), NT)

    copies = []

    def piece(one, two):
        shift = mm(gathered, jnp.concatenate([basis_ref[one, :], basis_ref[two, :]], axis=1), NT)
        out_ref[:, one] = (interior_ref[:, one].astype(F32) + shift[:loads]) * inverse_ref[:, one]
        out_ref[:, two] = (interior_ref[:, two].astype(F32) + shift[loads:]) * inverse_ref[:, two]

    def send(cut):
        copy = pltpu.make_async_copy(out_ref.at[:, cut], out_hbm.at[:, cut], sems.at[len(copies)])
        copy.start()
        copies.append(copy)

    faces = []
    for side, (_, _, exists) in enumerate(sides(width)):
        rest, shift = rests[side], shifts[side * loads : (side + 1) * loads]
        weights = jnp.concatenate([rest[loads * pieces + q : loads * pieces + q + 1] for q in range(pieces)], axis=1)
        scale = 1.0 / weights
        if exists is not None:
            scale = jnp.where(exists, scale, 0.0)
        inside = jnp.concatenate([rest[q * loads : (q + 1) * loads] for q in range(pieces)], axis=1)
        faces.append((inside + shift) * scale)
    odd = lax.rem(lax.axis_index("wide"), 2) == 1
    from_below, from_above = jnp.where(odd, faces[0], faces[1]), jnp.where(odd, faces[1], faces[0])

    quarter = width // 4
    ends = slice(0, quarter), slice(width - quarter, width)
    piece(*ends)
    out_ref[:, :NF] = out_ref[:, :NF] + from_below
    out_ref[:, width - NF :] = out_ref[:, width - NF :] + from_above
    send(ends[0])
    send(ends[1])
    piece(slice(quarter, half), slice(half, width - quarter))
    send(slice(quarter, width - quarter))
    for copy in copies:
        copy.wait()


def params(limit=LIMIT):
    return pltpu.CompilerParams(vmem_limit_bytes=limit)


def per_device(
    resid,
    mult,
    dirichlet_inv,
    fine_basis,
    fine_index,
    level2_inv,
    level2_basis,
    coarse_index,
    coarse_inv,
):
    loads, width = resid.shape
    blocks, size = dirichlet_inv.shape[0], dirichlet_inv.shape[1]
    wide, narrow = lax.axis_size("wide"), lax.axis_size("narrow")
    mult = mult.reshape(1, width)

    pieces = 3
    hbm = pl.BlockSpec(memory_space=pltpu.HBM)

    def pinned(*arrays):
        return [pltpu.with_memory_space_constraint(array, pltpu.HBM) for array in arrays]

    basis, weighted, inverse, send = pl.pallas_call(
        head_kernel,
        out_shape=(
            jax.ShapeDtypeStruct(fine_basis.shape, BF16),
            jax.ShapeDtypeStruct((loads, width), BF16),
            jax.ShapeDtypeStruct((1, width), F32),
            jax.ShapeDtypeStruct((narrow, 16, LANES), BF16),
        ),
        in_specs=[hbm] * 4,
        out_specs=(VMEM,) * 4,
        scratch_shapes=[
            pltpu.VMEM(resid.shape, F32),
            pltpu.VMEM(mult.shape, jnp.int32),
            pltpu.VMEM(fine_index.shape, jnp.int32),
            pltpu.SemaphoreType.DMA((3 + pieces,)),
        ],
        compiler_params=params(),
        name="head",
    )(*pinned(resid, mult, fine_basis, fine_index))
    parts = lax.all_to_all(send, "narrow", 0, 0)
    sixth = blocks // 6
    spans = tuple((at, sixth) for at in range(0, blocks, sixth))
    highs = coarse_inv.shape[1] // LANES
    interior, tiles = pl.pallas_call(
        functools.partial(interior_kernel, spans=spans),
        out_shape=(
            jax.ShapeDtypeStruct((loads, width), BF16),
            jax.ShapeDtypeStruct((highs // 2, LANES, LANES), BF16),
        ),
        input_output_aliases={0: 0},
        in_specs=[VMEM, hbm, hbm],
        out_specs=(VMEM, VMEM),
        scratch_shapes=[
            pltpu.VMEM(dirichlet_inv.shape, BF16),
            pltpu.VMEM(coarse_inv.shape, BF16),
            pltpu.SemaphoreType.DMA((len(spans) + 1,)),
        ],
        compiler_params=params(),
        cost_estimate=pl.CostEstimate(flops=2 * 16 * blocks * size * size, bytes_accessed=2 * blocks * size * size, transcendentals=0),
        name="interior",
    )(weighted, *pinned(dirichlet_inv, coarse_inv))

    near_rows = NF + LANES + REST + coarse_inv.size // LANES
    local, send, chosen, near, far = pl.pallas_call(
        level2_kernel,
        out_shape=(
            jax.ShapeDtypeStruct((loads, LANES), F32),
            jax.ShapeDtypeStruct((wide, 8, LANES), BF16),
            jax.ShapeDtypeStruct((LANES, LANES), BF16),
            jax.ShapeDtypeStruct((near_rows, LANES), BF16),
            jax.ShapeDtypeStruct((NF + LANES + REST, LANES), BF16),
        ),
        in_specs=[VMEM] * 9,
        out_specs=(VMEM,) * 5,
        scratch_shapes=[
            pltpu.VMEM((8, LANES), F32),
            pltpu.VMEM((REST, LANES), F32),
        ],
        compiler_params=params(),
        name="level2",
    )(parts, level2_inv, level2_basis, fine_index, coarse_index, interior, inverse, basis, tiles)
    far = lax.ppermute(far, "wide", [(i, (((i + 1) ^ 1) - 1) % wide) for i in range(wide)])
    near = lax.ppermute(near, "wide", [(i, i ^ 1) for i in range(wide)])
    packets = lax.all_to_all(send, "wide", 0, 0)
    packets, near, far = lax.optimization_barrier((packets, near, far))

    send, hot, owner = pl.pallas_call(
        functools.partial(coarse_kernel, width=width),
        out_shape=(
            jax.ShapeDtypeStruct((wide // 2, loads, LANES), BF16),
            jax.ShapeDtypeStruct((LANES, 3 * LANES), BF16),
            jax.ShapeDtypeStruct((8, 3 * LANES), F32),
        ),
        in_specs=[VMEM] * 4,
        out_specs=(VMEM,) * 3,
        compiler_params=params(),
        name="coarse",
    )(packets, tiles, coarse_index, near)
    cores = [[chip * 2 + core for chip in range(wide // 2)] for core in range(2)]
    corr = lax.all_to_all(send, "wide", 0, 0, axis_index_groups=cores)

    return pl.pallas_call(
        tail_kernel,
        out_shape=jax.ShapeDtypeStruct((loads, width), F32),
        in_specs=[VMEM] * 10,
        out_specs=hbm,
        scratch_shapes=[pltpu.VMEM((loads, width), F32), pltpu.SemaphoreType.DMA((3,))],
        compiler_params=params(),
        name="tail",
    )(corr, hot, owner, local, chosen, near, far, interior, inverse, basis)


def solution(mesh):
    placed = (
        P(None, ("wide", "narrow")),
        P(("wide", "narrow")),
        P(("wide", "narrow"), None, None),
        P(("wide", "narrow"), None),
        P(("wide", "narrow"), None),
        P("wide", None),
        P("wide", None),
        P("wide", None),
        P("wide", None),
    )
    return jax.shard_map(
        per_device,
        mesh=mesh,
        in_specs=placed,
        out_specs=P(None, ("wide", "narrow")),
        check_vma=False,
    )
```
